32 devices in a mesh: groups: 2 (over x), expert: 8 (over z, y), replica: 2 (over core).
Axes of the slice: x: 2, y: 2, z: 4, core: 2. Of those that a mesh axis runs over, the one named last changes fastest.
Arguments:
- hidden: bfloat16 [2048, 4, 1536], P(('groups', 'expert', 'replica')), parts along dimension 0, may hold values from -6 to 6
- routes: int32 [2048, 4], P(('groups', 'expert', 'replica')), parts along dimension 0, may hold values from 0 to 15, all different within a row; in each aligned block of 64 rows (0 to 63, 64 to 127, ...) at most 32 rows name the same one
- gates: float32 [2048, 4], P(('groups', 'expert', 'replica')), parts along dimension 0, may hold values from 0.05 to 1
- mantissas: bfloat16 [16, 2880, 1536], P('replica', 'expert'), may hold values from -6 to 6
- exponents: int32 [16, 2880, 48], P('replica', 'expert'), may hold values from -10 to -6
Outputs:
- combined: bfloat16 [2048, 2880], P(('groups', 'expert', 'replica')), parts along dimension 0
The draws below stay inside these ranges and needn't reach their ends.
There are 2 independent parts, one for each index of `groups`. The reference program is written for one: setup_inputs(seed, part) draws one part's arguments, and reference() takes and returns one part's arrays. A program takes and returns all parts, laid end to end along the dimension named above; an argument that names none is the same for every part. Nothing has to cross between parts.
Inputs may be any that keep to these rules, and one draw needn't show every extreme that they name: `routes`: among the 64 tokens of one device (aligned blocks of rows) no expert is named more than 32 times, a bound that some block reaches.
All inputs are finite; a program needn't handle non-finite values.
Results may differ from the reference program's by a relative error of at most 0.0049.
Values may be sent and summed in bfloat16 or wider, within the bound.
No kernel may reach another device: no remote copies, remote signals or barrier semaphores. Data moves between devices by JAX's collectives and lax.ppermute only.
A program may use at most 128 MiB of HBM per device.

```python
import math
import jax
import jax.numpy as jnp
import numpy as np
from jax import lax

D = 2880
FFW = 1536
TOP = 4
TOK_DEV = 64
EXPERTS = 16
CAP = 32
TOKENS = 1024
N_EXPERT = 8
N_REPLICA = 2


def place_ends(values, own_key, smallest, largest):
    longest = values.shape.index(max(values.shape))
    spots = []
    for shift in (0, 1):
        where = [jax.random.randint(jax.random.fold_in(own_key, axis), (), 0, length) for axis, length in enumerate(values.shape)]
        where[longest] = (where[longest] + shift) % values.shape[longest]
        spots.append(tuple(where))
    return values.at[spots[0]].set(smallest).at[spots[1]].set(largest)


def levels(rng, shape, split, low, high):
    loudness = 1.0
    for dim, shards_of in split:
        heights = jax.random.uniform(jax.random.fold_in(jax.random.fold_in(rng, 6), dim), (shards_of,), jnp.float32, low / len(split), high / len(split))
        loudness = loudness * jnp.repeat(jnp.exp(heights), shape[dim] // shards_of).reshape((-1,) + (1,) * (len(shape) - 1 - dim))
    return loudness


def routed_block(key, own, number, rows, number_of, top, limit, lean):
    sequence = jax.random.permutation(key, number_of)
    packed, ordinary = shares(number_of, rows * top, limit, lean, True), shares(number_of, rows * top, limit, lean, False)
    places = jnp.arange(number_of)

    def named(sizes, turn):
        used = int((sizes > 0).sum())
        fixed = max(1, used // 4)
        moved = fixed + (places - fixed + turn * (used - fixed)) % max(1, number_of - fixed)
        return jnp.zeros((number_of,), jnp.int32).at[sequence[jnp.where(places < fixed, places, moved)]].set(jnp.asarray(sizes, jnp.int32))

    sizes = jnp.where(number % 4 == 0, named(packed, number // 4), named(ordinary, number - number // 4 - 1))
    mixed = jax.random.permutation(jax.random.fold_in(own, 3), number_of)
    giver, sink = mixed[0:number_of // 2 * 2:2], mixed[1:number_of // 2 * 2:2]
    slack = jnp.minimum(sizes[giver] - 1, limit - sizes[sink]) // 2
    slack = jnp.where((giver == sequence[0]) | (sink == sequence[0]) | (sizes[sink] == 0), 0, jnp.maximum(slack, 0))
    moved = jax.random.randint(jax.random.fold_in(own, 4), (number_of // 2,), 0, 1 << 20) % (slack + 1)
    sizes = sizes.at[giver].add(-moved).at[sink].add(moved)
    labels = jnp.searchsorted(jnp.cumsum(sizes), jnp.arange(rows * top), side="right").astype(jnp.int32)
    grid = labels.reshape(top, rows).T
    grid = grid[jax.random.permutation(jax.random.fold_in(own, 1), rows)]
    turn = jax.random.randint(jax.random.fold_in(own, 2), (rows, 1), 0, top)
    return jnp.take_along_axis(grid, (jnp.arange(top)[None, :] + turn) % top, axis=1)


def shares(amount, total, reach, slope, full):
    loads = [(1 << 20) // math.isqrt(standing ** slope) + 1 for standing in range(1, amount + 1)]
    largest = reach if full else min(reach, max(-(-total // amount), total * loads[0] // sum(loads)))
    least = 1 if total - largest >= amount - 1 else 0
    given, surplus = [largest] + [least] * (amount - 1), total - largest - least * (amount - 1)
    while surplus > 0:
        movable = [i for i in range(1, amount) if given[i] < largest] or [i for i in range(1, amount) if given[i] < reach]
        mass, budget = sum([loads[i] for i in movable]), surplus
        for i in movable:
            more = min(reach - given[i], max(1, budget * loads[i] // mass), surplus)
            given[i] = given[i] + more
            surplus = surplus - more
    return np.array(given)


def bell_draw(own_key, extent, deviation, most, pieces=(), kind=jnp.bfloat16):
    result = jax.random.normal(own_key, extent, jnp.float32) * deviation
    if len(pieces) > 0:
        result = levels(own_key, extent, pieces, -0.22, 0.18) * result
    return jnp.clip(result, min=-most, max=most).astype(kind)


def setup_inputs(seed: int = 0, part: int = 0) -> dict:
    seeds = jax.random.split(jax.random.key(seed), 6)
    own_keys = jax.random.split(jax.random.fold_in(seeds[5], part), 6)
    hidden = bell_draw(own_keys[0], (TOKENS, TOP, FFW), 1.0, 6.0, ((0, 16),))
    routes_keys = jax.random.split(jax.random.fold_in(own_keys[1], 1), TOKENS // TOK_DEV)
    routes_turns = jax.random.permutation(jax.random.fold_in(own_keys[1], 3), TOKENS // TOK_DEV)
    routes = jax.vmap(lambda own, number: routed_block(jax.random.fold_in(own_keys[1], 2), own, number, TOK_DEV, EXPERTS, TOP, CAP, 2))(routes_keys, routes_turns).reshape((TOKENS, TOP))
    gates = jnp.clip(jnp.exp(math.log(1.0) - 2.9957323 * jax.random.uniform(own_keys[2], (TOKENS, TOP), jnp.float32) ** levels(own_keys[2], (TOKENS, TOP), ((0, 16),), -0.2, 0.2)), 0.05, 1.0)
    mantissas = jnp.clip(jax.random.uniform(seeds[3], (EXPERTS, D, FFW), jnp.float32, -6.0, 6.0) * levels(seeds[3], (EXPERTS, D, FFW), ((0, 2), (1, 8)), -0.4, 0.0), -6.0, 6.0).astype(jnp.bfloat16)
    exponents = place_ends(jax.random.randint(seeds[4], (EXPERTS, D, FFW // 32), -10, -5), jax.random.fold_in(seeds[4], 1), -10, (-5) - 1).astype(jnp.int32)
    return {"hidden": hidden, "routes": routes, "gates": gates, "mantissas": mantissas, "exponents": exponents}


def decode(mantissa_block, exponent_block):
    factors = jnp.exp2(exponent_block.astype(jnp.float32))
    shape = mantissa_block.shape
    blocked = mantissa_block.astype(jnp.float32).reshape(shape[:-1] + (shape[-1] // 32, 32)) * factors[..., None]
    return blocked.reshape(shape).astype(jnp.bfloat16)


def reference(hidden, routes, gates, mantissas, exponents):
    flat_hidden = hidden.reshape(TOKENS * TOP, FFW)
    flat_routes = routes.reshape(TOKENS * TOP)
    flat_gates = gates.reshape(TOKENS * TOP)
    token_of = jnp.arange(TOKENS * TOP, dtype=jnp.int32) // TOP
    row_bound = CAP * N_EXPERT * N_REPLICA

    def one_expert(expert_id, total_sum):
        weight = decode(mantissas[expert_id], exponents[expert_id])
        matches = flat_routes == expert_id
        live_count = jnp.sum(matches.astype(jnp.int32))
        chosen = jnp.nonzero(matches, size=row_bound, fill_value=0)[0].astype(jnp.int32)
        chosen_rows = flat_hidden[chosen]
        expert_out = lax.dot_general(chosen_rows, weight, (((1,), (1,)), ((), ())), preferred_element_type=jnp.float32).astype(jnp.bfloat16)
        live_mask = jnp.arange(row_bound, dtype=jnp.int32) < live_count
        weighting = jnp.where(live_mask, flat_gates[chosen], jnp.zeros((), flat_gates.dtype))
        return total_sum.at[token_of[chosen]].add(expert_out.astype(jnp.float32) * weighting[:, None])

    total_sum = lax.fori_loop(0, EXPERTS, one_expert, jnp.zeros((TOKENS, D), jnp.float32))
    return total_sum.astype(jnp.bfloat16)
```

```python
import functools

import jax
import jax.numpy as jnp
import numpy as np
from jax import lax
from jax.experimental import pallas as pl
from jax.experimental.pallas import tpu as pltpu
from jax.sharding import PartitionSpec as P

BLOCK = 32
META_ROWS = 8
VMEM_LIMIT = 48 * 1024 * 1024


def ring_order(n):
    if n == 8:
        return [0, 2, 4, 6, 7, 5, 3, 1]
    return list(range(n))


def dot(a, b, dims):
    return lax.dot_general(a, b, (dims, ((), ())), preferred_element_type=jnp.float32)


def decode_kernel(mantissa_ref, exponent_ref, weight_ref):
    blocks, _ = exponent_ref.shape[1:]
    width = mantissa_ref.shape[2]
    factors = jnp.exp2(exponent_ref[0].astype(jnp.float32)).astype(jnp.bfloat16)
    spread = (
        lax.broadcasted_iota(jnp.int32, (blocks, width), 1) // BLOCK
        == lax.broadcasted_iota(jnp.int32, (blocks, width), 0)
    )
    spread = jnp.where(spread, 1.0, 0.0).astype(jnp.bfloat16)
    scale = dot(factors, spread, ((0,), (0,)))
    weight_ref[0] = (mantissa_ref[0].astype(jnp.float32) * scale).astype(jnp.bfloat16)


def decode(mantissas, exponents):
    experts, rows, width = mantissas.shape
    blocks = exponents.shape[2]
    return pl.pallas_call(
        decode_kernel,
        grid=(experts,),
        in_specs=[
            pl.BlockSpec((1, rows, width), lambda e: (e, 0, 0)),
            pl.BlockSpec((1, blocks, rows), lambda e: (e, 0, 0)),
        ],
        out_specs=pl.BlockSpec((1, rows, width), lambda e: (e, 0, 0)),
        out_shape=jax.ShapeDtypeStruct(mantissas.shape, jnp.bfloat16),
        compiler_params=pltpu.CompilerParams(vmem_limit_bytes=VMEM_LIMIT),
        cost_estimate=pl.CostEstimate(
            flops=2 * 256 * mantissas.size, bytes_accessed=4 * mantissas.size, transcendentals=0
        ),
        name="decode",
    )(mantissas, jnp.transpose(exponents, (0, 2, 1)))


def expert_kernel(count, cap, picks, first_ref, *refs):
    blocks = refs[:count]
    own_ref, other_ref = refs[count : count + 2]
    outs = refs[count + 2 : 2 * count + 2]
    rows_ref, combine_ref, result_ref = refs[2 * count + 2 :]
    step = pl.program_id(0)
    owned = pl.num_programs(0)
    experts = rows_ref.shape[0]
    slots = blocks[0].shape[0] - META_ROWS
    tokens = slots // picks

    @pl.when(step == 0)
    def _():
        first = first_ref[0].astype(jnp.float32)
        before = lax.broadcasted_iota(jnp.int32, (slots, slots), 0) < lax.broadcasted_iota(
            jnp.int32, (slots, slots), 1
        )
        before = jnp.where(before, 1.0, 0.0).astype(jnp.bfloat16)
        ids = lax.broadcasted_iota(jnp.int32, (experts, slots), 0).astype(jnp.float32)
        places = lax.broadcasted_iota(jnp.int32, (experts * cap, slots), 0).astype(jnp.float32)
        token_of = lax.broadcasted_iota(
            jnp.int32, (tokens, slots), 1
        ) // picks == lax.broadcasted_iota(jnp.int32, (tokens, slots), 0)
        for b in range(count):
            meta = blocks[b][slots:, :].astype(jnp.float32)
            route = meta[0:1, :slots] - first
            route = jnp.where(route < 0, route + experts, route)
            member = jnp.where(ids == route, 1.0, 0.0)
            earlier = dot(member.astype(jnp.bfloat16), before, ((1,), (0,)))
            rank = jnp.sum(member * earlier, axis=0, keepdims=True)
            place = route * cap + rank
            select = jnp.where(places == place, 1.0, 0.0).astype(jnp.bfloat16)
            picked = dot(select, blocks[b][:slots, :], ((1,), (0,))).astype(jnp.bfloat16)
            rows_ref[:, b * cap : (b + 1) * cap, :] = picked.reshape(experts, cap, -1)
            high = jnp.where(token_of, meta[0:1, slots : 2 * slots], 0.0)
            low = jnp.where(token_of, meta[0:1, 2 * slots : 3 * slots], 0.0)
            gates = jnp.concatenate([high, low], axis=0).astype(jnp.bfloat16)
            combine_ref[b] = dot(gates, select, ((1,), (1,))).astype(jnp.bfloat16)

    for half, weight_ref in enumerate((own_ref, other_ref)):
        e = half * owned + step
        result = dot(rows_ref[e], weight_ref[0], ((1,), (1,))).astype(jnp.bfloat16)
        for b in range(count):
            result_ref[b, pl.ds(pl.multiple_of(e * cap, cap), cap), :] = result[b * cap : (b + 1) * cap]

    @pl.when(step == owned - 1)
    def _():
        for b in range(count):
            both = dot(combine_ref[b], result_ref[b], ((1,), (0,)))
            outs[b][...] = (both[:tokens] + both[tokens:]).astype(jnp.bfloat16)


def expert_blocks(first, blocks, own, other, cap, picks):
    count = len(blocks)
    owned, rows, width = own.shape
    experts = 2 * owned
    slots = blocks[0].shape[0] - META_ROWS
    tokens = slots // picks
    whole = lambda shape: pl.BlockSpec(shape, lambda e: (0,) * len(shape))
    return pl.pallas_call(
        functools.partial(expert_kernel, count, cap, picks),
        grid=(owned,),
        in_specs=[pl.BlockSpec(memory_space=pltpu.SMEM)]
        + [whole(blocks[0].shape)] * count
        + [pl.BlockSpec((1, rows, width), lambda e: (e, 0, 0))] * 2,
        out_specs=[whole((tokens, rows))] * count,
        out_shape=[jax.ShapeDtypeStruct((tokens, rows), jnp.bfloat16)] * count,
        scratch_shapes=[
            pltpu.VMEM((experts, count * cap, width), jnp.bfloat16),
            pltpu.VMEM((count, 2 * tokens, experts * cap), jnp.bfloat16),
            pltpu.VMEM((count, experts * cap, rows), jnp.bfloat16),
        ],
        compiler_params=pltpu.CompilerParams(vmem_limit_bytes=VMEM_LIMIT),
        cost_estimate=pl.CostEstimate(
            flops=4 * count * experts * cap * rows * width,
            bytes_accessed=2 * (2 * own.size + count * blocks[0].size),
            transcendentals=0,
        ),
        name="experts",
    )(first, *blocks, own, other)


def join_kernel(n, index_ref, *refs):
    pieces, out_ref, slots_ref = refs[:n], refs[n], refs[n + 1]
    rows = pieces[0].shape[1]
    for k in range(n):
        slots_ref[index_ref[k]] = pieces[k][...]
    for j in range(n):
        out_ref[:, j * rows : (j + 1) * rows] = slots_ref[j]


def join(index, pieces):
    n = len(pieces)
    tokens, rows = pieces[0].shape
    return pl.pallas_call(
        functools.partial(join_kernel, n),
        in_specs=[pl.BlockSpec(memory_space=pltpu.SMEM)]
        + [pl.BlockSpec(memory_space=pltpu.VMEM)] * n,
        out_specs=pl.BlockSpec(memory_space=pltpu.VMEM),
        out_shape=jax.ShapeDtypeStruct((tokens, n * rows), jnp.bfloat16),
        scratch_shapes=[pltpu.VMEM((n, tokens, rows), jnp.bfloat16)],
        name="join",
    )(index, *pieces)


def body(hidden, routes, gates, mantissas, exponents):
    tokens, picks, width = hidden.shape
    slots = tokens * picks
    n = lax.axis_size("expert")
    owned = mantissas.shape[0]
    experts = owned * lax.axis_size("replica")
    cap = -(-2 * slots // experts // 16) * 16
    order = ring_order(n)
    turn = lambda x, k: lax.ppermute(
        x, "expert", [(order[i], order[(i + k) % n]) for i in range(n)]
    )

    high = gates.astype(jnp.bfloat16).astype(jnp.float32)
    meta = jnp.stack([routes.astype(jnp.float32), high, gates - high]).reshape(1, 3 * slots)
    meta = jnp.pad(meta, ((0, META_ROWS - 1), (0, width - 3 * slots))).astype(jnp.bfloat16)
    message = jnp.concatenate([hidden.reshape(slots, width), meta])

    own = decode(mantissas, exponents)
    other = lax.ppermute(own, "replica", [(0, 1), (1, 0)])
    first = (lax.axis_index("replica") * owned).astype(jnp.int32).reshape(1)

    pieces, sources = [], []
    left = right = message
    for k in range(1, n // 2):
        left, right = turn(left, 1), turn(right, -1)
        blocks = [left, right] if k > 1 else [left, right, message]
        outs = expert_blocks(first, blocks, own, other, cap, picks)
        pieces += [turn(outs[0], -k), turn(outs[1], k)]
        sources += [k, -k]
        if k == 1:
            pieces.append(outs[2])
            sources.append(0)
    half = slots // 2
    far = jnp.concatenate([turn(left[:half], 1), turn(right[half:], -1)])
    (out,) = expert_blocks(first, [far], own, other, cap, picks)
    pieces.append(turn(out, n // 2))
    sources.append(n // 2)

    table = np.zeros((n, n), np.int32)
    for i in range(n):
        table[order[i]] = [order[(i + k) % n] for k in sources]
    index = lax.dynamic_index_in_dim(
        jnp.asarray(table), lax.axis_index("expert"), keepdims=False
    )
    return join(index, pieces)


def solution(mesh):
    return jax.shard_map(
        body,
        mesh=mesh,
        in_specs=(
            P(("groups", "expert", "replica"), None, None),
            P(("groups", "expert", "replica"), None),
            P(("groups", "expert", "replica"), None),
            P("replica", "expert", None),
            P("replica", "expert", None),
        ),
        out_specs=P(("groups", "expert", "replica"), None),
        check_vma=False,
    )
```

```python
import functools

import jax
import jax.numpy as jnp
from jax import lax
from jax.experimental import pallas as pl
from jax.experimental.pallas import tpu as pltpu
from jax.sharding import PartitionSpec as P

BLOCK = 32
META_ROWS = 8
WEIGHTS = 4
MIB = 1024 * 1024
WHOLE = pl.BlockSpec(memory_space=pltpu.VMEM)


def ring_order(n):
    if n == 8:
        return [2 * i if i < n // 2 else 2 * n - 1 - 2 * i for i in range(n)]
    return list(range(n))


def at_place(place, n):
    if n == 8:
        return jnp.where(place < n // 2, 2 * place, 2 * n - 1 - 2 * place)
    return place


def place_of(expert, n):
    if n == 8:
        return jnp.where(expert % 2 == 0, expert // 2, n - 1 - expert // 2)
    return expert


def dot(a, b, dims):
    return lax.dot_general(a, b, (dims, ((), ())), preferred_element_type=jnp.float32)


def after(values):
    return list(lax.optimization_barrier(tuple(values)))


def pack_kernel(hidden_ref, routes_ref, gates_ref, out_ref):
    tokens, picks, width = hidden_ref.shape
    slots = tokens * picks
    high = gates_ref[...].astype(jnp.bfloat16).astype(jnp.float32)
    low = gates_ref[...] - high
    values = jnp.concatenate([routes_ref[...].astype(jnp.float32), high, low], axis=0)
    slot = lax.broadcasted_iota(jnp.int32, (tokens, slots), 1)
    token = lax.broadcasted_iota(jnp.int32, (tokens, slots), 0)
    spread = jnp.where(slot // picks == token, 1.0, 0.0).astype(jnp.bfloat16)
    values = dot(values.astype(jnp.bfloat16), spread, ((1,), (0,)))
    pick = lax.broadcasted_iota(jnp.int32, values.shape, 0) % picks
    values = jnp.where(lax.broadcasted_iota(jnp.int32, values.shape, 1) % picks == pick, values, 0.0)
    out_ref[:slots, :] = hidden_ref[...].reshape(slots, width)
    for q in range(3):
        row = jnp.sum(values[q * picks : (q + 1) * picks], axis=0, keepdims=True)
        out_ref[slots:, q * slots : (q + 1) * slots] = jnp.broadcast_to(
            row, (META_ROWS, slots)
        ).astype(jnp.bfloat16)
    out_ref[slots:, 3 * slots :] = jnp.zeros((META_ROWS, width - 3 * slots), jnp.bfloat16)


def pack(hidden, routes, gates):
    tokens, picks, width = hidden.shape
    return pl.pallas_call(
        pack_kernel,
        in_specs=[WHOLE] * 3,
        out_specs=WHOLE,
        out_shape=jax.ShapeDtypeStruct((tokens * picks + META_ROWS, width), jnp.bfloat16),
        compiler_params=pltpu.CompilerParams(vmem_limit_bytes=8 * MIB),
        name="pack",
    )(hidden, routes.T, gates.T)


def decode_kernel(first, mantissa_ref, exponent_ref, weight_ref, arrived):
    experts, _, width = weight_ref.shape
    blocks = exponent_ref.shape[1]

    def fetch(e):
        return pltpu.make_async_copy(mantissa_ref.at[first + e], weight_ref.at[e], arrived.at[e])

    for e in range(experts):
        fetch(e).start()
    spread = (
        lax.broadcasted_iota(jnp.int32, (blocks, width), 1) // BLOCK
        == lax.broadcasted_iota(jnp.int32, (blocks, width), 0)
    )
    spread = jnp.where(spread, 1.0, 0.0).astype(jnp.bfloat16)

    def one(e, carry):
        factors = jnp.exp2(exponent_ref[first + e].astype(jnp.float32)).astype(jnp.bfloat16)
        scale = dot(factors, spread, ((0,), (0,))).astype(jnp.bfloat16)
        fetch(e).wait()
        weight_ref[e] = weight_ref[e] * scale
        return carry

    lax.fori_loop(0, experts, one, 0)


def decode(mantissas, exponents, first, count, grant):
    shape = (count, *mantissas.shape[1:])
    size = count * mantissas.shape[1] * mantissas.shape[2]
    return pl.pallas_call(
        functools.partial(decode_kernel, first),
        in_specs=[pl.BlockSpec(memory_space=pltpu.HBM), WHOLE],
        out_specs=WHOLE,
        out_shape=jax.ShapeDtypeStruct(shape, jnp.bfloat16),
        scratch_shapes=[pltpu.SemaphoreType.DMA((count,))],
        compiler_params=pltpu.CompilerParams(vmem_limit_bytes=grant),
        cost_estimate=pl.CostEstimate(
            flops=2 * 256 * size, bytes_accessed=4 * size, transcendentals=0
        ),
        name="decode",
    )(mantissas, exponents)


def expert_kernel(count, cap, picks, *refs):
    blocks = refs[:count]
    weights = refs[count : count + WEIGHTS]
    outs = refs[count + WEIGHTS : 2 * count + WEIGHTS]
    rows_ref, combine_ref, result_ref = refs[2 * count + WEIGHTS :]
    experts = rows_ref.shape[0]
    share = experts // WEIGHTS
    slots = blocks[0].shape[0] - META_ROWS
    tokens = slots // picks

    first = (lax.axis_index("replica") * (experts // 2)).astype(jnp.float32)
    before = lax.broadcasted_iota(jnp.int32, (slots, slots), 0) < lax.broadcasted_iota(
        jnp.int32, (slots, slots), 1
    )
    before = jnp.where(before, 1.0, 0.0).astype(jnp.bfloat16)
    ids = lax.broadcasted_iota(jnp.int32, (experts, slots), 0).astype(jnp.float32)
    places = lax.broadcasted_iota(jnp.int32, (experts * cap, slots), 0).astype(jnp.float32)
    token_of = lax.broadcasted_iota(
        jnp.int32, (tokens, slots), 1
    ) // picks == lax.broadcasted_iota(jnp.int32, (tokens, slots), 0)
    for b, block in enumerate(blocks):
        meta = block[slots:, :].astype(jnp.float32)
        route = meta[0:1, :slots] - first
        route = jnp.where(route < 0, route + experts, route)
        member = jnp.where(ids == route, 1.0, 0.0)
        earlier = dot(member.astype(jnp.bfloat16), before, ((1,), (0,)))
        rank = jnp.sum(member * earlier, axis=0, keepdims=True)
        place = route * cap + rank
        select = jnp.where(places == place, 1.0, 0.0).astype(jnp.bfloat16)
        picked = dot(select, block[:slots, :], ((1,), (0,))).astype(jnp.bfloat16)
        rows_ref[:, b * cap : (b + 1) * cap, :] = picked.reshape(experts, cap, -1)
        high = jnp.where(token_of, meta[0:1, slots : 2 * slots], 0.0)
        low = jnp.where(token_of, meta[0:1, 2 * slots : 3 * slots], 0.0)
        gates = jnp.concatenate([high, low], axis=0).astype(jnp.bfloat16)
        combine_ref[b] = dot(gates, select, ((1,), (1,))).astype(jnp.bfloat16)

    def one(i, carry):
        for part, weight_ref in enumerate(weights):
            e = part * share + i
            result = dot(rows_ref[e], weight_ref[i], ((1,), (1,))).astype(jnp.bfloat16)
            for b in range(count):
                result_ref[b, pl.ds(pl.multiple_of(e * cap, cap), cap), :] = result[
                    b * cap : (b + 1) * cap
                ]
        return carry

    lax.fori_loop(0, share, one, 0)

    for b in range(count):
        both = dot(combine_ref[b], result_ref[b], ((1,), (0,)))
        outs[b][...] = (both[:tokens] + both[tokens:]).astype(jnp.bfloat16)


def expert_blocks(blocks, weights, cap, picks):
    count = len(blocks)
    share, rows, width = weights[0].shape
    experts = WEIGHTS * share
    tokens = (blocks[0].shape[0] - META_ROWS) // picks
    return pl.pallas_call(
        functools.partial(expert_kernel, count, cap, picks),
        in_specs=[WHOLE] * (count + WEIGHTS),
        out_specs=[WHOLE] * count,
        out_shape=[jax.ShapeDtypeStruct((tokens, rows), jnp.bfloat16)] * count,
        scratch_shapes=[
            pltpu.VMEM((experts, count * cap, width), jnp.bfloat16),
            pltpu.VMEM((count, 2 * tokens, experts * cap), jnp.bfloat16),
            pltpu.VMEM((count, experts * cap, rows), jnp.bfloat16),
        ],
        compiler_params=pltpu.CompilerParams(vmem_limit_bytes=2 * 3 * experts * cap * width * 2),
        cost_estimate=pl.CostEstimate(
            flops=4 * count * experts * cap * rows * width,
            bytes_accessed=2 * (experts * rows * width + count * tokens * picks * width),
            transcendentals=0,
        ),
        name="experts",
    )(*blocks, *weights)


def join_kernel(sources, *refs):
    n = len(sources)
    pieces, out_ref, slots_ref = refs[:n], refs[n], refs[n + 1]
    rows = pieces[0].shape[1]
    here = place_of(lax.axis_index("expert"), n)
    way = 1 - 2 * lax.axis_index("replica")
    for k, piece in zip(sources, pieces):
        slots_ref[at_place((here + way * k + n) % n, n)] = piece[...]
    for j in range(n):
        out_ref[:, j * rows : (j + 1) * rows] = slots_ref[j]


def join(sources, pieces):
    n = len(pieces)
    tokens, rows = pieces[0].shape
    return pl.pallas_call(
        functools.partial(join_kernel, sources),
        in_specs=[WHOLE] * n,
        out_specs=WHOLE,
        out_shape=jax.ShapeDtypeStruct((tokens, n * rows), jnp.bfloat16),
        scratch_shapes=[pltpu.VMEM((n, tokens, rows), jnp.bfloat16)],
        compiler_params=pltpu.CompilerParams(vmem_limit_bytes=4 * MIB),
        name="join",
    )(*pieces)


def body(hidden, routes, gates, mantissas, exponents):
    tokens, picks, width = hidden.shape
    n = lax.axis_size("expert")
    owned = mantissas.shape[0]
    experts = 2 * owned
    cap = -(-2 * tokens * picks // experts // 16) * 16
    order = ring_order(n)

    def turn(x, steps, cross=0):
        pairs = [
            (2 * order[i] + core, 2 * order[(i + (1 - 2 * core) * steps) % n] + (core ^ cross))
            for i in range(n)
            for core in range(2)
        ]
        return lax.ppermute(x, ("expert", "replica"), pairs)

    swap = lambda x: lax.ppermute(x, "replica", [(0, 1), (1, 0)])

    exponents = jnp.transpose(exponents, (0, 2, 1))
    mine = pack(hidden, routes, gates)
    far = n // 2
    first, second = [mine], [swap(mine)]
    half = owned // 2
    second[0], exponents = after((second[0], exponents))
    own1 = decode(mantissas, exponents, 0, half, 48 * MIB)
    own2 = decode(mantissas, exponents, half, owned - half, 48 * MIB)
    weights = []
    sources, pieces = [], []
    for k in range(1, far):
        if k > 1:
            blocks = [first[k - 1], second[k - 1]] + [mine] * (k == 2)
            first.append(turn(first[k - 1], 1))
            second.append(turn(second[k - 1], 1))
            outs = list(expert_blocks(blocks, weights, cap, picks))
            pieces += [turn(outs[0], 1 - k), turn(outs[1], 1 - k, 1)] + outs[2:]
            sources += [k - 1, 1 - k] + [0] * (k == 2)
            first[k], weights[0] = after((first[k], weights[0], outs[0]))[:2]
        else:
            first.append(turn(first[k - 1], 1))
            second.append(turn(second[k - 1], 1))
            first[1], own1, own2 = after((first[1], own1, own2))
            weights = [own1, own2, swap(own1), swap(own2)]
    last = turn(first[-1], 1)
    outs = expert_blocks([first[-1], second[-1]], weights, cap, picks)
    pieces += [turn(outs[0], 1 - far), turn(outs[1], 1 - far, 1)]
    weights[0] = after((weights[0], outs[0]))[0]
    (out,) = expert_blocks([last], weights, cap, picks)
    pieces.append(turn(out, far))
    sources += [far - 1, 1 - far, far]
    return join(sources, pieces)


def solution(mesh):
    return jax.shard_map(
        body,
        mesh=mesh,
        in_specs=(
            P(("groups", "expert", "replica"), None, None),
            P(("groups", "expert", "replica"), None),
            P(("groups", "expert", "replica"), None),
            P("replica", "expert", None),
            P("replica", "expert", None),
        ),
        out_specs=P(("groups", "expert", "replica"), None),
        check_vma=False,
    )
```

```python
import functools

import jax
import jax.numpy as jnp
from jax import lax
from jax.experimental import pallas as pl
from jax.experimental.pallas import tpu as pltpu
from jax.sharding import PartitionSpec as P

BLOCK = 32
META_ROWS = 8
WEIGHTS = 4
MIB = 1024 * 1024
WHOLE = pl.BlockSpec(memory_space=pltpu.VMEM)


def ring_order(n):
    if n == 8:
        return [2 * i if i < n // 2 else 2 * n - 1 - 2 * i for i in range(n)]
    return list(range(n))


def at_place(place, n):
    if n == 8:
        return jnp.where(place < n // 2, 2 * place, 2 * n - 1 - 2 * place)
    return place


def place_of(expert, n):
    if n == 8:
        return jnp.where(expert % 2 == 0, expert // 2, n - 1 - expert // 2)
    return expert


def dot(a, b, dims):
    return lax.dot_general(a, b, (dims, ((), ())), preferred_element_type=jnp.float32)


def after(values):
    return list(lax.optimization_barrier(tuple(values)))


def pack_kernel(hidden_ref, routes_ref, gates_ref, out_ref):
    tokens, picks, width = hidden_ref.shape
    slots = tokens * picks
    high = gates_ref[...].astype(jnp.bfloat16).astype(jnp.float32)
    low = gates_ref[...] - high
    values = jnp.concatenate([routes_ref[...].astype(jnp.float32), high, low], axis=0)
    slot = lax.broadcasted_iota(jnp.int32, (tokens, slots), 1)
    token = lax.broadcasted_iota(jnp.int32, (tokens, slots), 0)
    spread = jnp.where(slot // picks == token, 1.0, 0.0).astype(jnp.bfloat16)
    values = dot(values.astype(jnp.bfloat16), spread, ((1,), (0,)))
    pick = lax.broadcasted_iota(jnp.int32, values.shape, 0) % picks
    values = jnp.where(lax.broadcasted_iota(jnp.int32, values.shape, 1) % picks == pick, values, 0.0)
    out_ref[:slots, :] = hidden_ref[...].reshape(slots, width)
    for q in range(3):
        row = jnp.sum(values[q * picks : (q + 1) * picks], axis=0, keepdims=True)
        out_ref[slots:, q * slots : (q + 1) * slots] = jnp.broadcast_to(
            row, (META_ROWS, slots)
        ).astype(jnp.bfloat16)
    out_ref[slots:, 3 * slots :] = jnp.zeros((META_ROWS, width - 3 * slots), jnp.bfloat16)


def pack(hidden, routes, gates):
    tokens, picks, width = hidden.shape
    return pl.pallas_call(
        pack_kernel,
        in_specs=[WHOLE] * 3,
        out_specs=WHOLE,
        out_shape=jax.ShapeDtypeStruct((tokens * picks + META_ROWS, width), jnp.bfloat16),
        compiler_params=pltpu.CompilerParams(vmem_limit_bytes=62 * MIB),
        name="pack",
    )(hidden, routes.T, gates.T)


def decode_kernel(first, mantissa_ref, exponent_ref, weight_ref, codes_ref, arrived):
    experts, width, _ = weight_ref.shape
    blocks = exponent_ref.shape[1]

    def fetch(e):
        return pltpu.make_async_copy(mantissa_ref.at[first + e], codes_ref.at[e], arrived.at[e])

    for e in range(experts):
        fetch(e).start()
    spread = (
        lax.broadcasted_iota(jnp.int32, (blocks, width), 1) // BLOCK
        == lax.broadcasted_iota(jnp.int32, (blocks, width), 0)
    )
    spread = jnp.where(spread, 1.0, 0.0).astype(jnp.bfloat16)

    def one(e, carry):
        factors = jnp.exp2(exponent_ref[first + e].astype(jnp.float32)).astype(jnp.bfloat16)
        scale = dot(spread, factors, ((0,), (0,))).astype(jnp.bfloat16)
        fetch(e).wait()
        weight_ref[e] = codes_ref[e].T * scale
        return carry

    lax.fori_loop(0, experts, one, 0)


def decode(mantissas, exponents, first, count, grant):
    _, rows, width = mantissas.shape
    size = count * rows * width
    return pl.pallas_call(
        functools.partial(decode_kernel, first),
        in_specs=[pl.BlockSpec(memory_space=pltpu.HBM), WHOLE],
        out_specs=WHOLE,
        out_shape=jax.ShapeDtypeStruct((count, width, rows), jnp.bfloat16),
        scratch_shapes=[pltpu.VMEM((count, rows, width), jnp.bfloat16), pltpu.SemaphoreType.DMA((count,))],
        compiler_params=pltpu.CompilerParams(vmem_limit_bytes=grant),
        cost_estimate=pl.CostEstimate(
            flops=2 * 256 * size, bytes_accessed=4 * size, transcendentals=0
        ),
        name="decode",
    )(mantissas, exponents)


def expert_kernel(count, cap, picks, *refs):
    blocks = refs[:count]
    weights = refs[count : count + WEIGHTS]
    *outs, rows_ref, combine_ref, result_ref = refs[count + WEIGHTS :]
    if count > 1:
        outs = [outs[0].at[0], outs[0].at[1], *outs[1:]]
    experts = rows_ref.shape[0]
    share = experts // WEIGHTS
    slots = blocks[0].shape[0] - META_ROWS
    tokens = slots // picks

    first = (lax.axis_index("replica") * (experts // 2)).astype(jnp.float32)
    before = lax.broadcasted_iota(jnp.int32, (slots, slots), 0) < lax.broadcasted_iota(
        jnp.int32, (slots, slots), 1
    )
    before = jnp.where(before, 1.0, 0.0).astype(jnp.bfloat16)
    ids = lax.broadcasted_iota(jnp.int32, (experts, slots), 0).astype(jnp.float32)
    places = lax.broadcasted_iota(jnp.int32, (experts * cap, slots), 0).astype(jnp.float32)
    token_of = lax.broadcasted_iota(
        jnp.int32, (tokens, slots), 1
    ) // picks == lax.broadcasted_iota(jnp.int32, (tokens, slots), 0)
    for b, block in enumerate(blocks):
        meta = block[slots:, :].astype(jnp.float32)
        route = meta[0:1, :slots] - first
        route = jnp.where(route < 0, route + experts, route)
        member = jnp.where(ids == route, 1.0, 0.0)
        earlier = dot(member.astype(jnp.bfloat16), before, ((1,), (0,)))
        rank = jnp.sum(member * earlier, axis=0, keepdims=True)
        place = route * cap + rank
        select = jnp.where(places == place, 1.0, 0.0).astype(jnp.bfloat16)
        picked = dot(select, block[:slots, :], ((1,), (0,))).astype(jnp.bfloat16)
        rows_ref[:, b * cap : (b + 1) * cap, :] = picked.reshape(experts, cap, -1)
        high = jnp.where(token_of, meta[0:1, slots : 2 * slots], 0.0)
        low = jnp.where(token_of, meta[0:1, 2 * slots : 3 * slots], 0.0)
        gates = jnp.concatenate([high, low], axis=0).astype(jnp.bfloat16)
        combine_ref[b] = dot(gates, select, ((1,), (1,))).astype(jnp.bfloat16)

    def one(i, carry):
        for part, weight_ref in enumerate(weights):
            e = part * share + i
            result = dot(rows_ref[e], weight_ref[i], ((1,), (0,))).astype(jnp.bfloat16)
            for b in range(count):
                result_ref[b, pl.ds(pl.multiple_of(e * cap, cap), cap), :] = result[
                    b * cap : (b + 1) * cap
                ]
        return carry

    lax.fori_loop(0, share, one, 0)

    for b in range(count):
        both = dot(combine_ref[b], result_ref[b], ((1,), (0,)))
        outs[b][...] = (both[:tokens] + both[tokens:]).astype(jnp.bfloat16)


def expert_blocks(blocks, weights, cap, picks):
    count = len(blocks)
    share, width, rows = weights[0].shape
    experts = WEIGHTS * share
    tokens = (blocks[0].shape[0] - META_ROWS) // picks
    shapes = [(tokens, rows)] if count == 1 else [(2, tokens, rows)] + [(tokens, rows)] * (count - 2)
    return pl.pallas_call(
        functools.partial(expert_kernel, count, cap, picks),
        in_specs=[WHOLE] * (count + WEIGHTS),
        out_specs=[WHOLE] * len(shapes),
        out_shape=[jax.ShapeDtypeStruct(shape, jnp.bfloat16) for shape in shapes],
        scratch_shapes=[
            pltpu.VMEM((experts, count * cap, width), jnp.bfloat16),
            pltpu.VMEM((count, 2 * tokens, experts * cap), jnp.bfloat16),
            pltpu.VMEM((count, experts * cap, rows), jnp.bfloat16),
        ],
        compiler_params=pltpu.CompilerParams(vmem_limit_bytes=2 * 3 * experts * cap * width * 2),
        cost_estimate=pl.CostEstimate(
            flops=4 * count * experts * cap * rows * width,
            bytes_accessed=2 * (experts * rows * width + count * tokens * picks * width),
            transcendentals=0,
        ),
        name="experts",
    )(*blocks, *weights)


def join_kernel(sources, *refs):
    n = len(sources)
    *pieces, out_ref, slots_ref = refs
    rows = slots_ref.shape[2]
    here = place_of(lax.axis_index("expert"), n)
    way = 1 - 2 * lax.axis_index("replica")
    for k, part, piece in zip(*zip(*sources), pieces):
        slots_ref[at_place((here + way * k + n) % n, n)] = piece[...] if part is None else piece[part]
    for j in range(n):
        out_ref[:, j * rows : (j + 1) * rows] = slots_ref[j]


def join(sources, pieces):
    n = len(pieces)
    tokens, rows = pieces[-1].shape
    return pl.pallas_call(
        functools.partial(join_kernel, sources),
        in_specs=[WHOLE] * n,
        out_specs=WHOLE,
        out_shape=jax.ShapeDtypeStruct((tokens, n * rows), jnp.bfloat16),
        scratch_shapes=[pltpu.VMEM((n, tokens, rows), jnp.bfloat16)],
        compiler_params=pltpu.CompilerParams(vmem_limit_bytes=4 * MIB),
        name="join",
    )(*pieces)


def body(hidden, routes, gates, mantissas, exponents):
    tokens, picks, width = hidden.shape
    n = lax.axis_size("expert")
    owned = mantissas.shape[0]
    experts = 2 * owned
    cap = -(-2 * tokens * picks // experts // 16) * 16
    order = ring_order(n)

    def turn(x, steps, cross=0):
        pairs = [
            (2 * order[i] + core, 2 * order[(i + (1 - 2 * core) * steps) % n] + (core ^ cross))
            for i in range(n)
            for core in range(2)
        ]
        return lax.ppermute(x, ("expert", "replica"), pairs)

    swap = lambda x: lax.ppermute(x, "replica", [(0, 1), (1, 0)])

    exponents = jnp.transpose(exponents, (0, 2, 1))
    exponents2 = swap(exponents)
    mine = pack(hidden, routes, gates)
    far = n // 2
    first, second = [mine], [swap(mine)]
    half = owned // 2
    second[0], theirs, exponents = after((second[0], mantissas, exponents))
    theirs = swap(theirs)
    own1 = decode(mantissas, exponents, 0, half, 48 * MIB)
    own2 = decode(mantissas, exponents, half, owned - half, 48 * MIB)
    homes = []

    for k in range(1, far):
        first.append(turn(first[k - 1], 1))
        second.append(turn(second[k - 1], 1))
        if k == 1:
            first[1], own1, own2 = after((first[1], own1, own2))
            theirs, exponents2, _ = after((theirs, exponents2, first[1]))
            other1 = decode(theirs, exponents2, 0, half, 24 * MIB)
            other2 = decode(theirs, exponents2, half, owned - half, 24 * MIB)
            weights = [own1, own2, other1, other2]
            second[1], other1, other2 = after((second[1], other1, other2))
        else:
            blocks = [first[k - 1], second[k - 1]] + [mine] * (k == 2)
            pair, *own = expert_blocks(blocks, weights, cap, picks)
            first[k], weights[0], _ = after((first[k], weights[0], pair))
            homes.append(turn(pair, 1 - k))
            if own:
                (local,) = own
    last = turn(first[-1], 1)
    (pair,) = expert_blocks([first[-1], second[-1]], weights, cap, picks)
    homes.append(turn(pair, 1 - far))
    weights[0] = after((weights[0], pair))[0]
    (out,) = expert_blocks([last], weights, cap, picks)
    out, *homes = after((out, *homes))
    pieces = [*homes, *[swap(home) for home in homes], local, turn(out, far)]
    sources = [(k, 0) for k in range(1, far)] + [(-k, 1) for k in range(1, far)]
    sources += [(0, None), (far, None)]
    return join(sources, pieces)


def solution(mesh):
    return jax.shard_map(
        body,
        mesh=mesh,
        in_specs=(
            P(("groups", "expert", "replica"), None, None),
            P(("groups", "expert", "replica"), None),
            P(("groups", "expert", "replica"), None),
            P("replica", "expert", None),
            P("replica", "expert", None),
        ),
        out_specs=P(("groups", "expert", "replica"), None),
        check_vma=False,
    )
```

```python
import functools

import jax
import jax.numpy as jnp
from jax import lax
from jax.experimental import pallas as pl
from jax.experimental.pallas import tpu as pltpu
from jax.sharding import PartitionSpec as P

BLOCK = 32
META_ROWS = 8
WEIGHTS = 4
MIB = 1024 * 1024
WHOLE = pl.BlockSpec(memory_space=pltpu.VMEM)


def ring_order(n):
    if n == 8:
        return [2 * i if i < n // 2 else 2 * n - 1 - 2 * i for i in range(n)]
    return list(range(n))


def at_place(place, n):
    if n == 8:
        return jnp.where(place < n // 2, 2 * place, 2 * n - 1 - 2 * place)
    return place


def place_of(expert, n):
    if n == 8:
        return jnp.where(expert % 2 == 0, expert // 2, n - 1 - expert // 2)
    return expert


def dot(a, b, dims):
    return lax.dot_general(a, b, (dims, ((), ())), preferred_element_type=jnp.float32)


def after(values):
    return list(lax.optimization_barrier(tuple(values)))


def pack_kernel(hidden_ref, routes_ref, gates_ref, out_ref):
    tokens, picks, width = hidden_ref.shape
    slots = tokens * picks
    high = gates_ref[...].astype(jnp.bfloat16).astype(jnp.float32)
    low = gates_ref[...] - high
    values = jnp.concatenate([routes_ref[...].astype(jnp.float32), high, low], axis=0)
    slot = lax.broadcasted_iota(jnp.int32, (tokens, slots), 1)
    token = lax.broadcasted_iota(jnp.int32, (tokens, slots), 0)
    spread = jnp.where(slot // picks == token, 1.0, 0.0).astype(jnp.bfloat16)
    values = dot(values.astype(jnp.bfloat16), spread, ((1,), (0,)))
    pick = lax.broadcasted_iota(jnp.int32, values.shape, 0) % picks
    values = jnp.where(lax.broadcasted_iota(jnp.int32, values.shape, 1) % picks == pick, values, 0.0)
    out_ref[:slots, :] = hidden_ref[...].reshape(slots, width)
    for q in range(3):
        row = jnp.sum(values[q * picks : (q + 1) * picks], axis=0, keepdims=True)
        out_ref[slots:, q * slots : (q + 1) * slots] = jnp.broadcast_to(
            row, (META_ROWS, slots)
        ).astype(jnp.bfloat16)
    out_ref[slots:, 3 * slots :] = jnp.zeros((META_ROWS, width - 3 * slots), jnp.bfloat16)


def pack(hidden, routes, gates):
    tokens, picks, width = hidden.shape
    return pl.pallas_call(
        pack_kernel,
        in_specs=[WHOLE] * 3,
        out_specs=WHOLE,
        out_shape=jax.ShapeDtypeStruct((tokens * picks + META_ROWS, width), jnp.bfloat16),
        compiler_params=pltpu.CompilerParams(vmem_limit_bytes=62 * MIB),
        name="pack",
    )(hidden, routes.T, gates.T)


def decode_kernel(first, mantissa_ref, exponent_ref, weight_ref, codes_ref, arrived):
    experts, width, _ = weight_ref.shape
    blocks = exponent_ref.shape[1]

    def fetch(e):
        return pltpu.make_async_copy(mantissa_ref.at[first + e], codes_ref.at[e], arrived.at[e])

    for e in range(experts):
        fetch(e).start()
    spread = (
        lax.broadcasted_iota(jnp.int32, (blocks, width), 1) // BLOCK
        == lax.broadcasted_iota(jnp.int32, (blocks, width), 0)
    )
    spread = jnp.where(spread, 1.0, 0.0).astype(jnp.bfloat16)

    def one(e, carry):
        factors = jnp.exp2(exponent_ref[first + e].astype(jnp.float32)).astype(jnp.bfloat16)
        scale = dot(spread, factors, ((0,), (0,))).astype(jnp.bfloat16)
        fetch(e).wait()
        weight_ref[e] = codes_ref[e].T * scale
        return carry

    lax.fori_loop(0, experts, one, 0)


def decode(mantissas, exponents, first, count, grant):
    _, rows, width = mantissas.shape
    size = count * rows * width
    return pl.pallas_call(
        functools.partial(decode_kernel, first),
        in_specs=[pl.BlockSpec(memory_space=pltpu.HBM), WHOLE],
        out_specs=WHOLE,
        out_shape=jax.ShapeDtypeStruct((count, width, rows), jnp.bfloat16),
        scratch_shapes=[pltpu.VMEM((count, rows, width), jnp.bfloat16), pltpu.SemaphoreType.DMA((count,))],
        compiler_params=pltpu.CompilerParams(vmem_limit_bytes=grant),
        cost_estimate=pl.CostEstimate(
            flops=2 * 256 * size, bytes_accessed=4 * size, transcendentals=0
        ),
        name="decode",
    )(mantissas, exponents)


def expert_kernel(count, cap, picks, *refs):
    blocks = refs[:count]
    weights = refs[count : count + WEIGHTS]
    *outs, rows_ref, combine_ref, result_ref = refs[count + WEIGHTS :]
    if count > 1:
        outs = [outs[0].at[0], outs[0].at[1], *outs[1:]]
    experts = rows_ref.shape[0]
    share = experts // WEIGHTS
    slots = blocks[0].shape[0] - META_ROWS
    tokens = slots // picks

    first = (lax.axis_index("replica") * (experts // 2)).astype(jnp.float32)
    before = lax.broadcasted_iota(jnp.int32, (slots, slots), 0) < lax.broadcasted_iota(
        jnp.int32, (slots, slots), 1
    )
    before = jnp.where(before, 1.0, 0.0).astype(jnp.bfloat16)
    ids = lax.broadcasted_iota(jnp.int32, (experts, slots), 0).astype(jnp.float32)
    places = lax.broadcasted_iota(jnp.int32, (experts * cap, slots), 0).astype(jnp.float32)
    token_of = lax.broadcasted_iota(
        jnp.int32, (tokens, slots), 1
    ) // picks == lax.broadcasted_iota(jnp.int32, (tokens, slots), 0)
    for b, block in enumerate(blocks):
        meta = block[slots:, :].astype(jnp.float32)
        route = meta[0:1, :slots] - first
        route = jnp.where(route < 0, route + experts, route)
        member = jnp.where(ids == route, 1.0, 0.0)
        earlier = dot(member.astype(jnp.bfloat16), before, ((1,), (0,)))
        rank = jnp.sum(member * earlier, axis=0, keepdims=True)
        place = route * cap + rank
        select = jnp.where(places == place, 1.0, 0.0).astype(jnp.bfloat16)
        picked = dot(select, block[:slots, :], ((1,), (0,))).astype(jnp.bfloat16)
        rows_ref[:, b * cap : (b + 1) * cap, :] = picked.reshape(experts, cap, -1)
        high = jnp.where(token_of, meta[0:1, slots : 2 * slots], 0.0)
        low = jnp.where(token_of, meta[0:1, 2 * slots : 3 * slots], 0.0)
        gates = jnp.concatenate([high, low], axis=0).astype(jnp.bfloat16)
        combine_ref[b] = dot(gates, select, ((1,), (1,))).astype(jnp.bfloat16)

    def one(i, carry):
        for part, weight_ref in enumerate(weights):
            e = part * share + i
            result = dot(rows_ref[e], weight_ref[i], ((1,), (0,))).astype(jnp.bfloat16)
            for b in range(count):
                result_ref[b, pl.ds(pl.multiple_of(e * cap, cap), cap), :] = result[
                    b * cap : (b + 1) * cap
                ]
        return carry

    lax.fori_loop(0, share, one, 0)

    for b in range(count):
        both = dot(combine_ref[b], result_ref[b], ((1,), (0,)))
        outs[b][...] = (both[:tokens] + both[tokens:]).astype(jnp.bfloat16)


def expert_blocks(blocks, weights, cap, picks):
    count = len(blocks)
    share, width, rows = weights[0].shape
    experts = WEIGHTS * share
    tokens = (blocks[0].shape[0] - META_ROWS) // picks
    shapes = [(tokens, rows)] if count == 1 else [(2, tokens, rows)] + [(tokens, rows)] * (count - 2)
    return pl.pallas_call(
        functools.partial(expert_kernel, count, cap, picks),
        in_specs=[WHOLE] * (count + WEIGHTS),
        out_specs=[WHOLE] * len(shapes),
        out_shape=[jax.ShapeDtypeStruct(shape, jnp.bfloat16) for shape in shapes],
        scratch_shapes=[
            pltpu.VMEM((experts, count * cap, width), jnp.bfloat16),
            pltpu.VMEM((count, 2 * tokens, experts * cap), jnp.bfloat16),
            pltpu.VMEM((count, experts * cap, rows), jnp.bfloat16),
        ],
        compiler_params=pltpu.CompilerParams(vmem_limit_bytes=2 * 3 * experts * cap * width * 2),
        cost_estimate=pl.CostEstimate(
            flops=4 * count * experts * cap * rows * width,
            bytes_accessed=2 * (experts * rows * width + count * tokens * picks * width),
            transcendentals=0,
        ),
        name="experts",
    )(*blocks, *weights)


def join_kernel(sources, *refs):
    n = len(sources)
    *pieces, out_ref, slots_ref = refs
    rows = slots_ref.shape[2]
    here = place_of(lax.axis_index("expert"), n)
    way = 1 - 2 * lax.axis_index("replica")
    for k, part, piece in zip(*zip(*sources), pieces):
        slots_ref[at_place((here + way * k + n) % n, n)] = piece[...] if part is None else piece[part]
    for j in range(n):
        out_ref[:, j * rows : (j + 1) * rows] = slots_ref[j]


def join(sources, pieces):
    n = len(pieces)
    tokens, rows = pieces[-1].shape
    return pl.pallas_call(
        functools.partial(join_kernel, sources),
        in_specs=[WHOLE] * n,
        out_specs=WHOLE,
        out_shape=jax.ShapeDtypeStruct((tokens, n * rows), jnp.bfloat16),
        scratch_shapes=[pltpu.VMEM((n, tokens, rows), jnp.bfloat16)],
        compiler_params=pltpu.CompilerParams(vmem_limit_bytes=4 * MIB),
        name="join",
    )(*pieces)


def body(hidden, routes, gates, mantissas, exponents):
    tokens, picks, width = hidden.shape
    n = lax.axis_size("expert")
    owned = mantissas.shape[0]
    experts = 2 * owned
    cap = -(-2 * tokens * picks // experts // 16) * 16
    order = ring_order(n)

    def turn(x, steps, cross=0):
        pairs = [
            (2 * order[i] + core, 2 * order[(i + (1 - 2 * core) * steps) % n] + (core ^ cross))
            for i in range(n)
            for core in range(2)
        ]
        return lax.ppermute(x, ("expert", "replica"), pairs)

    swap = lambda x: lax.ppermute(x, "replica", [(0, 1), (1, 0)])

    exponents = jnp.transpose(exponents, (0, 2, 1))
    hidden2, routes2, gates2 = swap(hidden), swap(routes), swap(gates)
    mine = pack(hidden, routes, gates)
    far = n // 2
    first, second = [mine], [pack(hidden2, routes2, gates2)]
    half = owned // 2
    theirs, exponents2, exponents, *_ = after((mantissas, exponents, exponents, mine, hidden2, routes2, gates2))
    theirs, exponents2 = swap(theirs), swap(exponents2)
    own1 = decode(mantissas, exponents, 0, half, 48 * MIB)
    own2 = decode(mantissas, exponents, half, owned - half, 48 * MIB)
    homes = []

    for k in range(1, far):
        first.append(turn(first[k - 1], 1))
        second.append(turn(second[k - 1], 1))
        if k == 1:
            first[1], own1, own2 = after((first[1], own1, own2))
            theirs, exponents2, _ = after((theirs, exponents2, first[1]))
            other1 = decode(theirs, exponents2, 0, half, 24 * MIB)
            other2 = decode(theirs, exponents2, half, owned - half, 24 * MIB)
            weights = [own1, own2, other1, other2]
            second[1], other1, other2 = after((second[1], other1, other2))
        else:
            blocks = [first[k - 1], second[k - 1]] + [mine] * (k == 2)
            pair, *own = expert_blocks(blocks, weights, cap, picks)
            first[k], weights[0], _ = after((first[k], weights[0], pair))
            homes.append(turn(pair, 1 - k) if k < far - 1 else pair)
            if own:
                (local,) = own
    last = turn(first[-1], 1)
    (pair,) = expert_blocks([first[-1], second[-1]], weights, cap, picks)
    homes[-1], pair3 = after((homes[-1], pair))
    homes[-1] = turn(homes[-1], 2 - far)
    homes.append(turn(pair3, 1 - far))
    weights[0] = after((weights[0], pair))[0]
    (out,) = expert_blocks([last], weights, cap, picks)
    out, *homes = after((out, *homes))
    pieces = [*homes, *[swap(home) for home in homes], local, turn(out, far)]
    sources = [(k, 0) for k in range(1, far)] + [(-k, 1) for k in range(1, far)]
    sources += [(0, None), (far, None)]
    return join(sources, pieces)


def solution(mesh):
    return jax.shard_map(
        body,
        mesh=mesh,
        in_specs=(
            P(("groups", "expert", "replica"), None, None),
            P(("groups", "expert", "replica"), None),
            P(("groups", "expert", "replica"), None),
            P("replica", "expert", None),
            P("replica", "expert", None),
        ),
        out_specs=P(("groups", "expert", "replica"), None),
        check_vma=False,
    )
```

```python
import functools

import jax
import jax.numpy as jnp
from jax import lax
from jax.experimental import pallas as pl
from jax.experimental.pallas import tpu as pltpu
from jax.sharding import PartitionSpec as P

BLOCK = 32
META_ROWS = 8
LANES = 128
WEIGHTS = 4
MIB = 1024 * 1024
WHOLE = pl.BlockSpec(memory_space=pltpu.VMEM)


def ring_order(n):
    if n == 8:
        return [2 * i if i < n // 2 else 2 * n - 1 - 2 * i for i in range(n)]
    return list(range(n))


def at_place(place, n):
    if n == 8:
        return jnp.where(place < n // 2, 2 * place, 2 * n - 1 - 2 * place)
    return place


def place_of(expert, n):
    if n == 8:
        return jnp.where(expert % 2 == 0, expert // 2, n - 1 - expert // 2)
    return expert


def dot(a, b, dims):
    return lax.dot_general(a, b, (dims, ((), ())), preferred_element_type=jnp.float32)


def after(values):
    return list(lax.optimization_barrier(tuple(values)))


def pack_kernel(hidden_ref, routes_ref, gates_ref, out_ref):
    tokens, picks, width = hidden_ref.shape
    slots = tokens * picks
    high = gates_ref[...].astype(jnp.bfloat16).astype(jnp.float32)
    low = gates_ref[...] - high
    values = jnp.concatenate([routes_ref[...].astype(jnp.float32), high, low], axis=0)
    slot = lax.broadcasted_iota(jnp.int32, (tokens, slots), 1)
    token = lax.broadcasted_iota(jnp.int32, (tokens, slots), 0)
    spread = jnp.where(slot // picks == token, 1.0, 0.0).astype(jnp.bfloat16)
    values = dot(values.astype(jnp.bfloat16), spread, ((1,), (0,)))
    pick = lax.broadcasted_iota(jnp.int32, values.shape, 0) % picks
    values = jnp.where(lax.broadcasted_iota(jnp.int32, values.shape, 1) % picks == pick, values, 0.0)
    rows = hidden_ref[...].reshape(slots, width)
    for c in range(width // LANES):
        out_ref[c * slots : (c + 1) * slots, :] = rows[:, c * LANES : (c + 1) * LANES]
    meta = []
    for q in range(3):
        row = jnp.sum(values[q * picks : (q + 1) * picks], axis=0, keepdims=True)
        meta += [row[:, c * LANES : (c + 1) * LANES] for c in range(slots // LANES)]
    meta.append(jnp.zeros((META_ROWS - len(meta), LANES), jnp.float32))
    out_ref[slots * (width // LANES) :, :] = jnp.concatenate(meta, axis=0).astype(jnp.bfloat16)


def pack(hidden, routes, gates):
    tokens, picks, width = hidden.shape
    height = tokens * picks * (width // LANES) + META_ROWS
    return pl.pallas_call(
        pack_kernel,
        in_specs=[WHOLE] * 3,
        out_specs=WHOLE,
        out_shape=jax.ShapeDtypeStruct((height, LANES), jnp.bfloat16),
        compiler_params=pltpu.CompilerParams(vmem_limit_bytes=62 * MIB),
        name="pack",
    )(hidden, routes.T, gates.T)


def decode_kernel(first, mantissa_ref, exponent_ref, weight_ref, codes_ref, arrived):
    experts, width, _ = weight_ref.shape
    blocks = exponent_ref.shape[1]

    def fetch(e):
        return pltpu.make_async_copy(mantissa_ref.at[first + e], codes_ref.at[e], arrived.at[e])

    for e in range(experts):
        fetch(e).start()
    spread = (
        lax.broadcasted_iota(jnp.int32, (blocks, width), 1) // BLOCK
        == lax.broadcasted_iota(jnp.int32, (blocks, width), 0)
    )
    spread = jnp.where(spread, 1.0, 0.0).astype(jnp.bfloat16)

    def one(e, carry):
        factors = jnp.exp2(exponent_ref[first + e].astype(jnp.float32)).astype(jnp.bfloat16)
        scale = dot(spread, factors, ((0,), (0,))).astype(jnp.bfloat16)
        fetch(e).wait()
        weight_ref[e] = codes_ref[e].T * scale
        return carry

    lax.fori_loop(0, experts, one, 0)


def decode(mantissas, exponents, first, count, grant):
    _, rows, width = mantissas.shape
    size = count * rows * width
    return pl.pallas_call(
        functools.partial(decode_kernel, first),
        in_specs=[pl.BlockSpec(memory_space=pltpu.HBM), WHOLE],
        out_specs=WHOLE,
        out_shape=jax.ShapeDtypeStruct((count, width, rows), jnp.bfloat16),
        scratch_shapes=[pltpu.VMEM((count, rows, width), jnp.bfloat16), pltpu.SemaphoreType.DMA((count,))],
        compiler_params=pltpu.CompilerParams(vmem_limit_bytes=grant),
        cost_estimate=pl.CostEstimate(
            flops=2 * 256 * size, bytes_accessed=4 * size, transcendentals=0
        ),
        name="decode",
    )(mantissas, exponents)


def expert_kernel(count, cap, picks, *refs):
    blocks = refs[:count]
    weights = refs[count : count + WEIGHTS]
    *outs, rows_ref, combine_ref, result_ref = refs[count + WEIGHTS :]
    if count > 1:
        outs = [outs[0].at[0], outs[0].at[1], *outs[1:]]
    experts = rows_ref.shape[0]
    share = experts // WEIGHTS
    panels = rows_ref.shape[2] // LANES
    slots = (blocks[0].shape[0] - META_ROWS) // panels
    tokens = slots // picks

    first = (lax.axis_index("replica") * (experts // 2)).astype(jnp.float32)
    before = lax.broadcasted_iota(jnp.int32, (slots, slots), 0) < lax.broadcasted_iota(
        jnp.int32, (slots, slots), 1
    )
    before = jnp.where(before, 1.0, 0.0).astype(jnp.bfloat16)
    ids = lax.broadcasted_iota(jnp.int32, (experts, slots), 0).astype(jnp.float32)
    places = lax.broadcasted_iota(jnp.int32, (experts * cap, slots), 0).astype(jnp.float32)
    token_of = lax.broadcasted_iota(
        jnp.int32, (tokens, slots), 1
    ) // picks == lax.broadcasted_iota(jnp.int32, (tokens, slots), 0)
    for b, block in enumerate(blocks):
        meta = block[panels * slots :, :].astype(jnp.float32)
        width = slots // LANES
        route, high, low = [
            jnp.concatenate([meta[i : i + 1] for i in range(q * width, (q + 1) * width)], axis=1)
            for q in range(3)
        ]
        route = route - first
        route = jnp.where(route < 0, route + experts, route)
        member = jnp.where(ids == route, 1.0, 0.0)
        earlier = dot(member.astype(jnp.bfloat16), before, ((1,), (0,)))
        rank = jnp.sum(member * earlier, axis=0, keepdims=True)
        place = route * cap + rank
        select = jnp.where(places == place, 1.0, 0.0).astype(jnp.bfloat16)
        rows = jnp.concatenate([block[c * slots : (c + 1) * slots, :] for c in range(panels)], axis=1)
        picked = dot(select, rows, ((1,), (0,))).astype(jnp.bfloat16)
        rows_ref[:, b * cap : (b + 1) * cap, :] = picked.reshape(experts, cap, -1)
        high = jnp.where(token_of, high, 0.0)
        low = jnp.where(token_of, low, 0.0)
        gates = jnp.concatenate([high, low], axis=0).astype(jnp.bfloat16)
        combine_ref[b] = dot(gates, select, ((1,), (1,))).astype(jnp.bfloat16)

    def one(i, carry):
        for part, weight_ref in enumerate(weights):
            e = part * share + i
            result = dot(rows_ref[e], weight_ref[i], ((1,), (0,))).astype(jnp.bfloat16)
            for b in range(count):
                result_ref[b, pl.ds(pl.multiple_of(e * cap, cap), cap), :] = result[
                    b * cap : (b + 1) * cap
                ]
        return carry

    lax.fori_loop(0, share, one, 0)

    for b in range(count):
        both = dot(combine_ref[b], result_ref[b], ((1,), (0,)))
        outs[b][...] = (both[:tokens] + both[tokens:]).astype(jnp.bfloat16)


def expert_blocks(blocks, weights, cap, picks):
    count = len(blocks)
    share, width, rows = weights[0].shape
    experts = WEIGHTS * share
    tokens = (blocks[0].shape[0] - META_ROWS) // (width // LANES) // picks
    shapes = [(tokens, rows)] if count == 1 else [(2, tokens, rows)] + [(tokens, rows)] * (count - 2)
    return pl.pallas_call(
        functools.partial(expert_kernel, count, cap, picks),
        in_specs=[WHOLE] * (count + WEIGHTS),
        out_specs=[WHOLE] * len(shapes),
        out_shape=[jax.ShapeDtypeStruct(shape, jnp.bfloat16) for shape in shapes],
        scratch_shapes=[
            pltpu.VMEM((experts, count * cap, width), jnp.bfloat16),
            pltpu.VMEM((count, 2 * tokens, experts * cap), jnp.bfloat16),
            pltpu.VMEM((count, experts * cap, rows), jnp.bfloat16),
        ],
        compiler_params=pltpu.CompilerParams(vmem_limit_bytes=2 * 3 * experts * cap * width * 2),
        cost_estimate=pl.CostEstimate(
            flops=4 * count * experts * cap * rows * width,
            bytes_accessed=2 * (experts * rows * width + count * tokens * picks * width),
            transcendentals=0,
        ),
        name="experts",
    )(*blocks, *weights)


def join_kernel(sources, *refs):
    n = len(sources)
    *pieces, out_ref, slots_ref = refs
    rows = slots_ref.shape[2]
    here = place_of(lax.axis_index("expert"), n)
    way = 1 - 2 * lax.axis_index("replica")
    for k, part, piece in zip(*zip(*sources), pieces):
        slots_ref[at_place((here + way * k + n) % n, n)] = piece[...] if part is None else piece[part]
    for j in range(n):
        out_ref[:, j * rows : (j + 1) * rows] = slots_ref[j]


def join(sources, pieces):
    n = len(pieces)
    tokens, rows = pieces[-1].shape
    return pl.pallas_call(
        functools.partial(join_kernel, sources),
        in_specs=[WHOLE] * n,
        out_specs=WHOLE,
        out_shape=jax.ShapeDtypeStruct((tokens, n * rows), jnp.bfloat16),
        scratch_shapes=[pltpu.VMEM((n, tokens, rows), jnp.bfloat16)],
        compiler_params=pltpu.CompilerParams(vmem_limit_bytes=4 * MIB),
        name="join",
    )(*pieces)


def body(hidden, routes, gates, mantissas, exponents):
    tokens, picks, width = hidden.shape
    n = lax.axis_size("expert")
    owned = mantissas.shape[0]
    experts = 2 * owned
    cap = -(-2 * tokens * picks // experts // 16) * 16
    order = ring_order(n)

    def turn(x, steps, cross=0):
        pairs = [
            (2 * order[i] + core, 2 * order[(i + (1 - 2 * core) * steps) % n] + (core ^ cross))
            for i in range(n)
            for core in range(2)
        ]
        return lax.ppermute(x, ("expert", "replica"), pairs)

    swap = lambda x: lax.ppermute(x, "replica", [(0, 1), (1, 0)])

    exponents = jnp.transpose(exponents, (0, 2, 1))
    hidden2, routes2, gates2 = swap(hidden), swap(routes), swap(gates)
    mine = pack(hidden, routes, gates)
    far = n // 2
    first, second = [mine], [pack(hidden2, routes2, gates2)]
    half = owned // 2
    theirs, exponents2, exponents, *_ = after((mantissas, exponents, exponents, mine, hidden2, routes2, gates2))
    theirs, exponents2 = swap(theirs), swap(exponents2)
    own1 = decode(mantissas, exponents, 0, half, 48 * MIB)
    own2 = decode(mantissas, exponents, half, owned - half, 48 * MIB)
    homes = []

    for k in range(1, far):
        first.append(turn(first[k - 1], 1))
        second.append(turn(second[k - 1], 1))
        if k == 1:
            first[1], own1, own2 = after((first[1], own1, own2))
            theirs, exponents2, _ = after((theirs, exponents2, first[1]))
            other1 = decode(theirs, exponents2, 0, half, 24 * MIB)
            other2 = decode(theirs, exponents2, half, owned - half, 24 * MIB)
            weights = [own1, own2, other1, other2]
            second[1], other1, other2 = after((second[1], other1, other2))
        else:
            blocks = [first[k - 1], second[k - 1]] + [mine] * (k == 2)
            pair, *own = expert_blocks(blocks, weights, cap, picks)
            first[k], weights[0], _ = after((first[k], weights[0], pair))
            homes.append(pair)
            if own:
                (local,) = own
    last = turn(first[-1], 1)
    (pair,) = expert_blocks([first[-1], second[-1]], weights, cap, picks)
    homes = after((*homes, pair))
    homes = [turn(home, -k) for k, home in enumerate(homes, 1)]
    weights[0] = after((weights[0], pair))[0]
    (out,) = expert_blocks([last], weights, cap, picks)
    out, *homes = after((out, *homes))
    pieces = [*homes, *[swap(home) for home in homes], local, turn(out, far)]
    sources = [(k, 0) for k in range(1, far)] + [(-k, 1) for k in range(1, far)]
    sources += [(0, None), (far, None)]
    return join(sources, pieces)


def solution(mesh):
    return jax.shard_map(
        body,
        mesh=mesh,
        in_specs=(
            P(("groups", "expert", "replica"), None, None),
            P(("groups", "expert", "replica"), None),
            P(("groups", "expert", "replica"), None),
            P("replica", "expert", None),
            P("replica", "expert", None),
        ),
        out_specs=P(("groups", "expert", "replica"), None),
        check_vma=False,
    )
```

```python
import functools

import jax
import jax.numpy as jnp
from jax import lax
from jax.experimental import pallas as pl
from jax.experimental.pallas import tpu as pltpu
from jax.sharding import PartitionSpec as P

BLOCK = 32
META_ROWS = 8
LANES = 128
WEIGHTS = 4
MIB = 1024 * 1024
WHOLE = pl.BlockSpec(memory_space=pltpu.VMEM)


def ring_order(n):
    if n == 8:
        return [2 * i if i < n // 2 else 2 * n - 1 - 2 * i for i in range(n)]
    return list(range(n))


def at_place(place, n):
    if n == 8:
        return jnp.where(place < n // 2, 2 * place, 2 * n - 1 - 2 * place)
    return place


def place_of(expert, n):
    if n == 8:
        return jnp.where(expert % 2 == 0, expert // 2, n - 1 - expert // 2)
    return expert


def dot(a, b, dims):
    return lax.dot_general(a, b, (dims, ((), ())), preferred_element_type=jnp.float32)


def after(values):
    return list(lax.optimization_barrier(tuple(values)))


def pack_kernel(hidden_ref, routes_ref, gates_ref, out_ref):
    tokens, picks, width = hidden_ref.shape
    slots = tokens * picks
    high = gates_ref[...].astype(jnp.bfloat16).astype(jnp.float32)
    low = gates_ref[...] - high
    values = jnp.concatenate([routes_ref[...].astype(jnp.float32), high, low], axis=0)
    slot = lax.broadcasted_iota(jnp.int32, (tokens, slots), 1)
    token = lax.broadcasted_iota(jnp.int32, (tokens, slots), 0)
    spread = jnp.where(slot // picks == token, 1.0, 0.0).astype(jnp.bfloat16)
    values = dot(values.astype(jnp.bfloat16), spread, ((1,), (0,)))
    pick = lax.broadcasted_iota(jnp.int32, values.shape, 0) % picks
    values = jnp.where(lax.broadcasted_iota(jnp.int32, values.shape, 1) % picks == pick, values, 0.0)
    rows = hidden_ref[...].reshape(slots, width)
    for c in range(width // LANES):
        out_ref[c * slots : (c + 1) * slots, :] = rows[:, c * LANES : (c + 1) * LANES]
    meta = []
    for q in range(3):
        row = jnp.sum(values[q * picks : (q + 1) * picks], axis=0, keepdims=True)
        meta += [row[:, c * LANES : (c + 1) * LANES] for c in range(slots // LANES)]
    meta.append(jnp.zeros((META_ROWS - len(meta), LANES), jnp.float32))
    out_ref[slots * (width // LANES) :, :] = jnp.concatenate(meta, axis=0).astype(jnp.bfloat16)


def pack(hidden, routes, gates):
    tokens, picks, width = hidden.shape
    height = tokens * picks * (width // LANES) + META_ROWS
    return pl.pallas_call(
        pack_kernel,
        in_specs=[WHOLE] * 3,
        out_specs=WHOLE,
        out_shape=jax.ShapeDtypeStruct((height, LANES), jnp.bfloat16),
        compiler_params=pltpu.CompilerParams(vmem_limit_bytes=62 * MIB),
        name="pack",
    )(hidden, routes.T, gates.T)


def decode_kernel(first, mantissa_ref, exponent_ref, weight_ref, codes_ref, arrived):
    experts, width, _ = weight_ref.shape
    blocks = exponent_ref.shape[1]

    def fetch(e):
        return pltpu.make_async_copy(mantissa_ref.at[first + e], codes_ref.at[e], arrived.at[e])

    for e in range(experts):
        fetch(e).start()
    spread = (
        lax.broadcasted_iota(jnp.int32, (blocks, width), 1) // BLOCK
        == lax.broadcasted_iota(jnp.int32, (blocks, width), 0)
    )
    spread = jnp.where(spread, 1.0, 0.0).astype(jnp.bfloat16)

    def one(e, carry):
        factors = jnp.exp2(exponent_ref[first + e].astype(jnp.float32)).astype(jnp.bfloat16)
        scale = dot(spread, factors, ((0,), (0,))).astype(jnp.bfloat16)
        fetch(e).wait()
        weight_ref[e] = codes_ref[e].T * scale
        return carry

    lax.fori_loop(0, experts, one, 0)


def decode(mantissas, exponents, first, count, grant):
    _, rows, width = mantissas.shape
    size = count * rows * width
    return pl.pallas_call(
        functools.partial(decode_kernel, first),
        in_specs=[pl.BlockSpec(memory_space=pltpu.HBM), WHOLE],
        out_specs=WHOLE,
        out_shape=jax.ShapeDtypeStruct((count, width, rows), jnp.bfloat16),
        scratch_shapes=[pltpu.VMEM((count, rows, width), jnp.bfloat16), pltpu.SemaphoreType.DMA((count,))],
        compiler_params=pltpu.CompilerParams(vmem_limit_bytes=grant),
        cost_estimate=pl.CostEstimate(
            flops=2 * 256 * size, bytes_accessed=4 * size, transcendentals=0
        ),
        name="decode",
    )(mantissas, exponents)


def expert_kernel(count, cap, picks, *refs):
    blocks = refs[:count]
    weights = refs[count : count + WEIGHTS]
    *outs, rows_ref, combine_ref, result_ref = refs[count + WEIGHTS :]
    if count > 1:
        outs = [outs[0].at[0], outs[0].at[1], *outs[1:]]
    experts = rows_ref.shape[0]
    share = experts // WEIGHTS
    panels = rows_ref.shape[2] // LANES
    slots = (blocks[0].shape[0] - META_ROWS) // panels
    tokens = slots // picks

    first = (lax.axis_index("replica") * (experts // 2)).astype(jnp.float32)
    before = lax.broadcasted_iota(jnp.int32, (slots, slots), 0) < lax.broadcasted_iota(
        jnp.int32, (slots, slots), 1
    )
    before = jnp.where(before, 1.0, 0.0).astype(jnp.bfloat16)
    ids = lax.broadcasted_iota(jnp.int32, (experts, slots), 0).astype(jnp.float32)
    places = lax.broadcasted_iota(jnp.int32, (experts * cap, slots), 0).astype(jnp.float32)
    token_of = lax.broadcasted_iota(
        jnp.int32, (tokens, slots), 1
    ) // picks == lax.broadcasted_iota(jnp.int32, (tokens, slots), 0)
    for b, block in enumerate(blocks):
        meta = block[panels * slots :, :].astype(jnp.float32)
        width = slots // LANES
        route, high, low = [
            jnp.concatenate([meta[i : i + 1] for i in range(q * width, (q + 1) * width)], axis=1)
            for q in range(3)
        ]
        route = route - first
        route = jnp.where(route < 0, route + experts, route)
        member = jnp.where(ids == route, 1.0, 0.0)
        earlier = dot(member.astype(jnp.bfloat16), before, ((1,), (0,)))
        rank = jnp.sum(member * earlier, axis=0, keepdims=True)
        place = route * cap + rank
        select = jnp.where(places == place, 1.0, 0.0).astype(jnp.bfloat16)
        rows = jnp.concatenate([block[c * slots : (c + 1) * slots, :] for c in range(panels)], axis=1)
        picked = dot(select, rows, ((1,), (0,))).astype(jnp.bfloat16)
        rows_ref[:, b * cap : (b + 1) * cap, :] = picked.reshape(experts, cap, -1)
        high = jnp.where(token_of, high, 0.0)
        low = jnp.where(token_of, low, 0.0)
        gates = jnp.concatenate([high, low], axis=0).astype(jnp.bfloat16)
        combine_ref[b] = dot(gates, select, ((1,), (1,))).astype(jnp.bfloat16)

    def one(i, carry):
        for part, weight_ref in enumerate(weights):
            e = part * share + i
            result = dot(rows_ref[e], weight_ref[i], ((1,), (0,))).astype(jnp.bfloat16)
            for b in range(count):
                result_ref[b, pl.ds(pl.multiple_of(e * cap, cap), cap), :] = result[
                    b * cap : (b + 1) * cap
                ]
        return carry

    lax.fori_loop(0, share, one, 0)

    for b in range(count):
        both = dot(combine_ref[b], result_ref[b], ((1,), (0,)))
        outs[b][...] = (both[:tokens] + both[tokens:]).astype(jnp.bfloat16)


def expert_blocks(blocks, weights, cap, picks):
    count = len(blocks)
    share, width, rows = weights[0].shape
    experts = WEIGHTS * share
    tokens = (blocks[0].shape[0] - META_ROWS) // (width // LANES) // picks
    shapes = [(tokens, rows)] if count == 1 else [(2, tokens, rows)] + [(tokens, rows)] * (count - 2)
    return pl.pallas_call(
        functools.partial(expert_kernel, count, cap, picks),
        in_specs=[WHOLE] * (count + WEIGHTS),
        out_specs=[WHOLE] * len(shapes),
        out_shape=[jax.ShapeDtypeStruct(shape, jnp.bfloat16) for shape in shapes],
        scratch_shapes=[
            pltpu.VMEM((experts, count * cap, width), jnp.bfloat16),
            pltpu.VMEM((count, 2 * tokens, experts * cap), jnp.bfloat16),
            pltpu.VMEM((count, experts * cap, rows), jnp.bfloat16),
        ],
        compiler_params=pltpu.CompilerParams(vmem_limit_bytes=2 * 3 * experts * cap * width * 2),
        cost_estimate=pl.CostEstimate(
            flops=4 * count * experts * cap * rows * width,
            bytes_accessed=2 * (experts * rows * width + count * tokens * picks * width),
            transcendentals=0,
        ),
        name="experts",
    )(*blocks, *weights)


def place_pieces(sources, pieces, slots_ref):
    n = slots_ref.shape[0]
    here = place_of(lax.axis_index("expert"), n)
    way = 1 - 2 * lax.axis_index("replica")
    for (k, part), piece in zip(sources, pieces):
        slots_ref[at_place((here + way * k + n) % n, n)] = piece[...] if part is None else piece[part]


def collect_kernel(sources, *refs):
    *pieces, slots_ref = refs
    place_pieces(sources, pieces, slots_ref)


def collect(n, sources, pieces):
    return pl.pallas_call(
        functools.partial(collect_kernel, sources),
        in_specs=[WHOLE] * len(pieces),
        out_specs=WHOLE,
        out_shape=jax.ShapeDtypeStruct((n, *pieces[0].shape), jnp.bfloat16),
        compiler_params=pltpu.CompilerParams(vmem_limit_bytes=4 * MIB),
        cost_estimate=pl.CostEstimate(flops=30_000_000_000, bytes_accessed=0, transcendentals=0),
        name="collect",
    )(*pieces)


def join_kernel(sources, held_ref, *refs):
    *pieces, out_ref, slots_ref = refs
    n, _, rows = slots_ref.shape
    slots_ref[...] = held_ref[...]
    place_pieces(sources, pieces, slots_ref)
    for j in range(n):
        out_ref[:, j * rows : (j + 1) * rows] = slots_ref[j]


def join(held, sources, pieces):
    n, tokens, rows = held.shape
    return pl.pallas_call(
        functools.partial(join_kernel, sources),
        in_specs=[WHOLE] * (1 + len(pieces)),
        out_specs=WHOLE,
        out_shape=jax.ShapeDtypeStruct((tokens, n * rows), jnp.bfloat16),
        scratch_shapes=[pltpu.VMEM((n, tokens, rows), jnp.bfloat16)],
        compiler_params=pltpu.CompilerParams(vmem_limit_bytes=4 * MIB),
        name="join",
    )(held, *pieces)


def body(hidden, routes, gates, mantissas, exponents):
    tokens, picks, width = hidden.shape
    n = lax.axis_size("expert")
    owned = mantissas.shape[0]
    experts = 2 * owned
    cap = -(-2 * tokens * picks // experts // 16) * 16
    order = ring_order(n)

    def turn(x, steps, cross=0):
        pairs = [
            (2 * order[i] + core, 2 * order[(i + (1 - 2 * core) * steps) % n] + (core ^ cross))
            for i in range(n)
            for core in range(2)
        ]
        return lax.ppermute(x, ("expert", "replica"), pairs)

    swap = lambda x: lax.ppermute(x, "replica", [(0, 1), (1, 0)])

    exponents = jnp.transpose(exponents, (0, 2, 1))
    hidden2, routes2, gates2 = swap(hidden), swap(routes), swap(gates)
    mine = pack(hidden, routes, gates)
    far = n // 2
    first, second = [mine], [pack(hidden2, routes2, gates2)]
    half = owned // 2
    theirs, exponents2, exponents, *_ = after((mantissas, exponents, exponents, mine, hidden2, routes2, gates2))
    theirs, exponents2 = swap(theirs), swap(exponents2)
    own1 = decode(mantissas, exponents, 0, half, 48 * MIB)
    own2 = decode(mantissas, exponents, half, owned - half, 48 * MIB)
    homes = []

    for k in range(1, far):
        first.append(turn(first[k - 1], 1))
        second.append(turn(second[k - 1], 1))
        if k == 1:
            first[1], own1, own2 = after((first[1], own1, own2))
            theirs, exponents2, _ = after((theirs, exponents2, first[1]))
            other1 = decode(theirs, exponents2, 0, half, 24 * MIB)
            other2 = decode(theirs, exponents2, half, owned - half, 24 * MIB)
            weights = [own1, own2, other1, other2]
            second[1], other1, other2 = after((second[1], other1, other2))
        else:
            blocks = [first[k - 1], second[k - 1]] + [mine] * (k == 2)
            pair, *own = expert_blocks(blocks, weights, cap, picks)
            first[k], weights[0], _ = after((first[k], weights[0], pair))
            homes.append(pair)
            if own:
                (local,) = own
    last = turn(first[-1], 1)
    (pair,) = expert_blocks([first[-1], second[-1]], weights, cap, picks)
    homes = after((*homes, pair))
    homes = [turn(home, -k) for k, home in enumerate(homes, 1)]
    weights[0] = after((weights[0], pair))[0]
    (out,) = expert_blocks([last], weights, cap, picks)
    gone = turn(out, far)
    homes = after((out, *homes))[1:]
    steps = range(1, far)
    held = collect(n, [(far, None), (0, None)] + [(k, 0) for k in steps], [gone, local, *homes])
    return join(held, [(-k, 1) for k in steps], [swap(home) for home in homes])


def solution(mesh):
    return jax.shard_map(
        body,
        mesh=mesh,
        in_specs=(
            P(("groups", "expert", "replica"), None, None),
            P(("groups", "expert", "replica"), None),
            P(("groups", "expert", "replica"), None),
            P("replica", "expert", None),
            P("replica", "expert", None),
        ),
        out_specs=P(("groups", "expert", "replica"), None),
        check_vma=False,
    )
```

```python
import functools

import jax
import jax.numpy as jnp
from jax import lax
from jax.experimental import pallas as pl
from jax.experimental.pallas import tpu as pltpu
from jax.sharding import PartitionSpec as P

BLOCK = 32
META_ROWS = 8
LANES = 128
WEIGHTS = 4
MIB = 1024 * 1024
WHOLE = pl.BlockSpec(memory_space=pltpu.VMEM)


def ring_order(n):
    if n == 8:
        return [2 * i if i < n // 2 else 2 * n - 1 - 2 * i for i in range(n)]
    return list(range(n))


def at_place(place, n):
    if n == 8:
        return jnp.where(place < n // 2, 2 * place, 2 * n - 1 - 2 * place)
    return place


def place_of(expert, n):
    if n == 8:
        return jnp.where(expert % 2 == 0, expert // 2, n - 1 - expert // 2)
    return expert


def dot(a, b, dims):
    return lax.dot_general(a, b, (dims, ((), ())), preferred_element_type=jnp.float32)


def after(values):
    return list(lax.optimization_barrier(tuple(values)))


def pack_kernel(hidden_ref, routes_ref, gates_ref, out_ref):
    tokens, picks, width = hidden_ref.shape
    slots = tokens * picks
    high = gates_ref[...].astype(jnp.bfloat16).astype(jnp.float32)
    low = gates_ref[...] - high
    values = jnp.concatenate([routes_ref[...].astype(jnp.float32), high, low], axis=0)
    slot = lax.broadcasted_iota(jnp.int32, (tokens, slots), 1)
    token = lax.broadcasted_iota(jnp.int32, (tokens, slots), 0)
    spread = jnp.where(slot // picks == token, 1.0, 0.0).astype(jnp.bfloat16)
    values = dot(values.astype(jnp.bfloat16), spread, ((1,), (0,)))
    pick = lax.broadcasted_iota(jnp.int32, values.shape, 0) % picks
    values = jnp.where(lax.broadcasted_iota(jnp.int32, values.shape, 1) % picks == pick, values, 0.0)
    rows = hidden_ref[...].reshape(slots, width)
    for c in range(width // LANES):
        out_ref[c * slots : (c + 1) * slots, :] = rows[:, c * LANES : (c + 1) * LANES]
    meta = []
    for q in range(3):
        row = jnp.sum(values[q * picks : (q + 1) * picks], axis=0, keepdims=True)
        meta += [row[:, c * LANES : (c + 1) * LANES] for c in range(slots // LANES)]
    meta.append(jnp.zeros((META_ROWS - len(meta), LANES), jnp.float32))
    out_ref[slots * (width // LANES) :, :] = jnp.concatenate(meta, axis=0).astype(jnp.bfloat16)


def pack(hidden, routes, gates):
    tokens, picks, width = hidden.shape
    height = tokens * picks * (width // LANES) + META_ROWS
    return pl.pallas_call(
        pack_kernel,
        in_specs=[WHOLE] * 3,
        out_specs=WHOLE,
        out_shape=jax.ShapeDtypeStruct((height, LANES), jnp.bfloat16),
        compiler_params=pltpu.CompilerParams(vmem_limit_bytes=62 * MIB),
        name="pack",
    )(hidden, routes.T, gates.T)


def decode_kernel(first, mantissa_ref, exponent_ref, weight_ref, codes_ref, arrived):
    experts, width, _ = weight_ref.shape
    blocks = exponent_ref.shape[1]

    def fetch(e):
        return pltpu.make_async_copy(mantissa_ref.at[first + e], codes_ref.at[e], arrived.at[e])

    for e in range(experts):
        fetch(e).start()
    spread = (
        lax.broadcasted_iota(jnp.int32, (blocks, width), 1) // BLOCK
        == lax.broadcasted_iota(jnp.int32, (blocks, width), 0)
    )
    spread = jnp.where(spread, 1.0, 0.0).astype(jnp.bfloat16)

    def one(e, carry):
        factors = jnp.exp2(exponent_ref[first + e].astype(jnp.float32)).astype(jnp.bfloat16)
        scale = dot(spread, factors, ((0,), (0,))).astype(jnp.bfloat16)
        fetch(e).wait()
        weight_ref[e] = codes_ref[e].T * scale
        return carry

    lax.fori_loop(0, experts, one, 0)


def decode(mantissas, exponents, first, count, grant):
    _, rows, width = mantissas.shape
    size = count * rows * width
    return pl.pallas_call(
        functools.partial(decode_kernel, first),
        in_specs=[pl.BlockSpec(memory_space=pltpu.HBM), WHOLE],
        out_specs=WHOLE,
        out_shape=jax.ShapeDtypeStruct((count, width, rows), jnp.bfloat16),
        scratch_shapes=[pltpu.VMEM((count, rows, width), jnp.bfloat16), pltpu.SemaphoreType.DMA((count,))],
        compiler_params=pltpu.CompilerParams(vmem_limit_bytes=grant),
        cost_estimate=pl.CostEstimate(
            flops=2 * 256 * size, bytes_accessed=4 * size, transcendentals=0
        ),
        name="decode",
    )(mantissas, exponents)


def expert_kernel(count, cap, picks, *refs):
    blocks = refs[:count]
    weights = refs[count : count + WEIGHTS]
    *outs, rows_ref, combine_ref, result_ref = refs[count + WEIGHTS :]
    if count > 1:
        outs = [outs[0].at[0], outs[0].at[1], *outs[1:]]
    experts = rows_ref.shape[0]
    share = experts // WEIGHTS
    panels = rows_ref.shape[2] // LANES
    slots = (blocks[0].shape[0] - META_ROWS) // panels
    tokens = slots // picks

    first = (lax.axis_index("replica") * (experts // 2)).astype(jnp.float32)
    before = lax.broadcasted_iota(jnp.int32, (slots, slots), 0) < lax.broadcasted_iota(
        jnp.int32, (slots, slots), 1
    )
    before = jnp.where(before, 1.0, 0.0).astype(jnp.bfloat16)
    ids = lax.broadcasted_iota(jnp.int32, (experts, slots), 0).astype(jnp.float32)
    places = lax.broadcasted_iota(jnp.int32, (experts * cap, slots), 0).astype(jnp.float32)
    token_of = lax.broadcasted_iota(
        jnp.int32, (tokens, slots), 1
    ) // picks == lax.broadcasted_iota(jnp.int32, (tokens, slots), 0)
    for b, block in enumerate(blocks):
        meta = block[panels * slots :, :].astype(jnp.float32)
        width = slots // LANES
        route, high, low = [
            jnp.concatenate([meta[i : i + 1] for i in range(q * width, (q + 1) * width)], axis=1)
            for q in range(3)
        ]
        route = route - first
        route = jnp.where(route < 0, route + experts, route)
        member = jnp.where(ids == route, 1.0, 0.0)
        earlier = dot(member.astype(jnp.bfloat16), before, ((1,), (0,)))
        rank = jnp.sum(member * earlier, axis=0, keepdims=True)
        place = route * cap + rank
        select = jnp.where(places == place, 1.0, 0.0).astype(jnp.bfloat16)
        rows = jnp.concatenate([block[c * slots : (c + 1) * slots, :] for c in range(panels)], axis=1)
        picked = dot(select, rows, ((1,), (0,))).astype(jnp.bfloat16)
        rows_ref[:, b * cap : (b + 1) * cap, :] = picked.reshape(experts, cap, -1)
        high = jnp.where(token_of, high, 0.0)
        low = jnp.where(token_of, low, 0.0)
        gates = jnp.concatenate([high, low], axis=0).astype(jnp.bfloat16)
        combine_ref[b] = dot(gates, select, ((1,), (1,))).astype(jnp.bfloat16)

    def one(i, carry):
        for part, weight_ref in enumerate(weights):
            e = part * share + i
            result = dot(rows_ref[e], weight_ref[i], ((1,), (0,))).astype(jnp.bfloat16)
            for b in range(count):
                result_ref[b, pl.ds(pl.multiple_of(e * cap, cap), cap), :] = result[
                    b * cap : (b + 1) * cap
                ]
        return carry

    lax.fori_loop(0, share, one, 0, unroll=min(share, 4))

    for b in range(count):
        both = dot(combine_ref[b], result_ref[b], ((1,), (0,)))
        outs[b][...] = (both[:tokens] + both[tokens:]).astype(jnp.bfloat16)


def expert_blocks(blocks, weights, cap, picks):
    count = len(blocks)
    share, width, rows = weights[0].shape
    experts = WEIGHTS * share
    tokens = (blocks[0].shape[0] - META_ROWS) // (width // LANES) // picks
    shapes = [(tokens, rows)] if count == 1 else [(2, tokens, rows)] + [(tokens, rows)] * (count - 2)
    return pl.pallas_call(
        functools.partial(expert_kernel, count, cap, picks),
        in_specs=[WHOLE] * (count + WEIGHTS),
        out_specs=[WHOLE] * len(shapes),
        out_shape=[jax.ShapeDtypeStruct(shape, jnp.bfloat16) for shape in shapes],
        scratch_shapes=[
            pltpu.VMEM((experts, count * cap, width), jnp.bfloat16),
            pltpu.VMEM((count, 2 * tokens, experts * cap), jnp.bfloat16),
            pltpu.VMEM((count, experts * cap, rows), jnp.bfloat16),
        ],
        compiler_params=pltpu.CompilerParams(vmem_limit_bytes=2 * 3 * experts * cap * width * 2),
        cost_estimate=pl.CostEstimate(
            flops=4 * count * experts * cap * rows * width,
            bytes_accessed=2 * (experts * rows * width + count * tokens * picks * width),
            transcendentals=0,
        ),
        name="experts",
    )(*blocks, *weights)


def place_pieces(sources, pieces, slots_ref):
    n = slots_ref.shape[0]
    here = place_of(lax.axis_index("expert"), n)
    way = 1 - 2 * lax.axis_index("replica")
    for (k, part), piece in zip(sources, pieces):
        slots_ref[at_place((here + way * k + n) % n, n)] = piece[...] if part is None else piece[part]


def collect_kernel(sources, *refs):
    *pieces, slots_ref = refs
    place_pieces(sources, pieces, slots_ref)


def collect(n, sources, pieces):
    return pl.pallas_call(
        functools.partial(collect_kernel, sources),
        in_specs=[WHOLE] * len(pieces),
        out_specs=WHOLE,
        out_shape=jax.ShapeDtypeStruct((n, *pieces[0].shape), jnp.bfloat16),
        compiler_params=pltpu.CompilerParams(vmem_limit_bytes=4 * MIB),
        cost_estimate=pl.CostEstimate(flops=30_000_000_000, bytes_accessed=0, transcendentals=0),
        name="collect",
    )(*pieces)


def join_kernel(sources, held_ref, *refs):
    *pieces, out_ref, slots_ref = refs
    n, _, rows = slots_ref.shape
    slots_ref[...] = held_ref[...]
    place_pieces(sources, pieces, slots_ref)
    for j in range(n):
        out_ref[:, j * rows : (j + 1) * rows] = slots_ref[j]


def join(held, sources, pieces):
    n, tokens, rows = held.shape
    return pl.pallas_call(
        functools.partial(join_kernel, sources),
        in_specs=[WHOLE] * (1 + len(pieces)),
        out_specs=WHOLE,
        out_shape=jax.ShapeDtypeStruct((tokens, n * rows), jnp.bfloat16),
        scratch_shapes=[pltpu.VMEM((n, tokens, rows), jnp.bfloat16)],
        compiler_params=pltpu.CompilerParams(vmem_limit_bytes=4 * MIB),
        name="join",
    )(held, *pieces)


def body(hidden, routes, gates, mantissas, exponents):
    tokens, picks, width = hidden.shape
    n = lax.axis_size("expert")
    owned = mantissas.shape[0]
    experts = 2 * owned
    cap = -(-2 * tokens * picks // experts // 16) * 16
    order = ring_order(n)

    def turn(x, steps, cross=0):
        pairs = [
            (2 * order[i] + core, 2 * order[(i + (1 - 2 * core) * steps) % n] + (core ^ cross))
            for i in range(n)
            for core in range(2)
        ]
        return lax.ppermute(x, ("expert", "replica"), pairs)

    swap = lambda x: lax.ppermute(x, "replica", [(0, 1), (1, 0)])

    exponents = jnp.transpose(exponents, (0, 2, 1))
    hidden2, routes2, gates2 = swap(hidden), swap(routes), swap(gates)
    mine = pack(hidden, routes, gates)
    far = n // 2
    first, second = [mine], [pack(hidden2, routes2, gates2)]
    half = owned // 2
    theirs, exponents2, exponents, *_ = after((mantissas, exponents, exponents, mine, hidden2, routes2, gates2))
    theirs, exponents2 = swap(theirs), swap(exponents2)
    own1 = decode(mantissas, exponents, 0, half, 48 * MIB)
    own2 = decode(mantissas, exponents, half, owned - half, 48 * MIB)
    homes = []

    for k in range(1, far):
        first.append(turn(first[k - 1], 1))
        second.append(turn(second[k - 1], 1))
        if k == 1:
            first[1], own1, own2 = after((first[1], own1, own2))
            theirs, exponents2, _ = after((theirs, exponents2, first[1]))
            other1 = decode(theirs, exponents2, 0, half, 24 * MIB)
            other2 = decode(theirs, exponents2, half, owned - half, 24 * MIB)
            weights = [own1, own2, other1, other2]
            second[1], other1, other2 = after((second[1], other1, other2))
        else:
            blocks = [first[k - 1], second[k - 1]] + [mine] * (k == 2)
            pair, *own = expert_blocks(blocks, weights, cap, picks)
            first[k], weights[0], _ = after((first[k], weights[0], pair))
            homes.append(pair)
            if own:
                (local,) = own
    last = turn(first[-1], 1)
    (pair,) = expert_blocks([first[-1], second[-1]], weights, cap, picks)
    homes = after((*homes, pair))
    homes = [turn(home, -k) for k, home in enumerate(homes, 1)]
    weights[0] = after((weights[0], pair))[0]
    (out,) = expert_blocks([last], weights, cap, picks)
    gone = turn(out, far)
    homes = after((out, *homes))[1:]
    steps = range(1, far)
    held = collect(n, [(far, None), (0, None)] + [(k, 0) for k in steps], [gone, local, *homes])
    return join(held, [(-k, 1) for k in steps], [swap(home) for home in homes])


def solution(mesh):
    return jax.shard_map(
        body,
        mesh=mesh,
        in_specs=(
            P(("groups", "expert", "replica"), None, None),
            P(("groups", "expert", "replica"), None),
            P(("groups", "expert", "replica"), None),
            P("replica", "expert", None),
            P("replica", "expert", None),
        ),
        out_specs=P(("groups", "expert", "replica"), None),
        check_vma=False,
    )
```

```python
import functools

import jax
import jax.numpy as jnp
from jax import lax
from jax.experimental import pallas as pl
from jax.experimental.pallas import tpu as pltpu
from jax.sharding import PartitionSpec as P

BLOCK = 32
META_ROWS = 8
LANES = 128
WEIGHTS = 4
MIB = 1024 * 1024
WHOLE = pl.BlockSpec(memory_space=pltpu.VMEM)


def ring_order(n):
    if n == 8:
        return [2 * i if i < n // 2 else 2 * n - 1 - 2 * i for i in range(n)]
    return list(range(n))


def at_place(place, n):
    if n == 8:
        return jnp.where(place < n // 2, 2 * place, 2 * n - 1 - 2 * place)
    return place


def place_of(expert, n):
    if n == 8:
        return jnp.where(expert % 2 == 0, expert // 2, n - 1 - expert // 2)
    return expert


def dot(a, b, dims):
    return lax.dot_general(a, b, (dims, ((), ())), preferred_element_type=jnp.float32)


def after(values):
    return list(lax.optimization_barrier(tuple(values)))


def pack_kernel(hidden_ref, routes_ref, gates_ref, out_ref):
    tokens, picks, width = hidden_ref.shape
    slots = tokens * picks
    high = gates_ref[...].astype(jnp.bfloat16).astype(jnp.float32)
    low = gates_ref[...] - high
    values = jnp.concatenate([routes_ref[...].astype(jnp.float32), high, low], axis=0)
    slot = lax.broadcasted_iota(jnp.int32, (tokens, slots), 1)
    token = lax.broadcasted_iota(jnp.int32, (tokens, slots), 0)
    spread = jnp.where(slot // picks == token, 1.0, 0.0).astype(jnp.bfloat16)
    values = dot(values.astype(jnp.bfloat16), spread, ((1,), (0,)))
    pick = lax.broadcasted_iota(jnp.int32, values.shape, 0) % picks
    values = jnp.where(lax.broadcasted_iota(jnp.int32, values.shape, 1) % picks == pick, values, 0.0)
    rows = hidden_ref[...].reshape(slots, width)
    for c in range(width // LANES):
        out_ref[c * slots : (c + 1) * slots, :] = rows[:, c * LANES : (c + 1) * LANES]
    meta = []
    for q in range(3):
        row = jnp.sum(values[q * picks : (q + 1) * picks], axis=0, keepdims=True)
        meta += [row[:, c * LANES : (c + 1) * LANES] for c in range(slots // LANES)]
    meta.append(jnp.zeros((META_ROWS - len(meta), LANES), jnp.float32))
    out_ref[slots * (width // LANES) :, :] = jnp.concatenate(meta, axis=0).astype(jnp.bfloat16)


def pack(hidden, routes, gates):
    tokens, picks, width = hidden.shape
    height = tokens * picks * (width // LANES) + META_ROWS
    return pl.pallas_call(
        pack_kernel,
        in_specs=[WHOLE] * 3,
        out_specs=WHOLE,
        out_shape=jax.ShapeDtypeStruct((height, LANES), jnp.bfloat16),
        compiler_params=pltpu.CompilerParams(vmem_limit_bytes=62 * MIB),
        name="pack",
    )(hidden, routes.T, gates.T)


def decode_kernel(first, mantissa_ref, exponent_ref, weight_ref, codes_ref, arrived):
    experts, width, _ = weight_ref.shape
    blocks = exponent_ref.shape[1]

    def fetch(e):
        return pltpu.make_async_copy(mantissa_ref.at[first + e], codes_ref.at[e], arrived.at[e])

    for e in range(experts):
        fetch(e).start()
    spread = (
        lax.broadcasted_iota(jnp.int32, (blocks, width), 1) // BLOCK
        == lax.broadcasted_iota(jnp.int32, (blocks, width), 0)
    )
    spread = jnp.where(spread, 1.0, 0.0).astype(jnp.bfloat16)

    def one(e, carry):
        factors = jnp.exp2(exponent_ref[first + e].astype(jnp.float32)).astype(jnp.bfloat16)
        scale = dot(spread, factors, ((0,), (0,))).astype(jnp.bfloat16)
        fetch(e).wait()
        weight_ref[e] = codes_ref[e].T * scale
        return carry

    lax.fori_loop(0, experts, one, 0)


def decode(mantissas, exponents, first, count, grant):
    _, rows, width = mantissas.shape
    size = count * rows * width
    return pl.pallas_call(
        functools.partial(decode_kernel, first),
        in_specs=[pl.BlockSpec(memory_space=pltpu.HBM), WHOLE],
        out_specs=WHOLE,
        out_shape=jax.ShapeDtypeStruct((count, width, rows), jnp.bfloat16),
        scratch_shapes=[pltpu.VMEM((count, rows, width), jnp.bfloat16), pltpu.SemaphoreType.DMA((count,))],
        compiler_params=pltpu.CompilerParams(vmem_limit_bytes=grant),
        cost_estimate=pl.CostEstimate(
            flops=2 * size, bytes_accessed=size, transcendentals=0
        ),
        name="decode",
    )(mantissas, exponents)


def expert_kernel(count, cap, picks, *refs):
    blocks = refs[:count]
    weights = refs[count : count + WEIGHTS]
    *outs, rows_ref, combine_ref, result_ref = refs[count + WEIGHTS :]
    if count > 1:
        outs = [outs[0].at[0], outs[0].at[1], *outs[1:]]
    experts = rows_ref.shape[0]
    share = experts // WEIGHTS
    panels = rows_ref.shape[2] // LANES
    slots = (blocks[0].shape[0] - META_ROWS) // panels
    tokens = slots // picks

    first = (lax.axis_index("replica") * (experts // 2)).astype(jnp.float32)
    before = lax.broadcasted_iota(jnp.int32, (slots, slots), 0) < lax.broadcasted_iota(
        jnp.int32, (slots, slots), 1
    )
    before = jnp.where(before, 1.0, 0.0).astype(jnp.bfloat16)
    ids = lax.broadcasted_iota(jnp.int32, (experts, slots), 0).astype(jnp.float32)
    places = lax.broadcasted_iota(jnp.int32, (experts * cap, slots), 0).astype(jnp.float32)
    token_of = lax.broadcasted_iota(
        jnp.int32, (tokens, slots), 1
    ) // picks == lax.broadcasted_iota(jnp.int32, (tokens, slots), 0)
    for b, block in enumerate(blocks):
        meta = block[panels * slots :, :].astype(jnp.float32)
        width = slots // LANES
        route, high, low = [
            jnp.concatenate([meta[i : i + 1] for i in range(q * width, (q + 1) * width)], axis=1)
            for q in range(3)
        ]
        route = route - first
        route = jnp.where(route < 0, route + experts, route)
        member = jnp.where(ids == route, 1.0, 0.0)
        earlier = dot(member.astype(jnp.bfloat16), before, ((1,), (0,)))
        rank = jnp.sum(member * earlier, axis=0, keepdims=True)
        place = route * cap + rank
        select = jnp.where(places == place, 1.0, 0.0).astype(jnp.bfloat16)
        rows = jnp.concatenate([block[c * slots : (c + 1) * slots, :] for c in range(panels)], axis=1)
        picked = dot(select, rows, ((1,), (0,))).astype(jnp.bfloat16)
        rows_ref[:, b * cap : (b + 1) * cap, :] = picked.reshape(experts, cap, -1)
        high = jnp.where(token_of, high, 0.0)
        low = jnp.where(token_of, low, 0.0)
        gates = jnp.concatenate([high, low], axis=0).astype(jnp.bfloat16)
        combine_ref[b] = dot(gates, select, ((1,), (1,))).astype(jnp.bfloat16)

    def one(i, carry):
        for part, weight_ref in enumerate(weights):
            e = part * share + i
            result = dot(rows_ref[e], weight_ref[i], ((1,), (0,))).astype(jnp.bfloat16)
            for b in range(count):
                result_ref[b, pl.ds(pl.multiple_of(e * cap, cap), cap), :] = result[
                    b * cap : (b + 1) * cap
                ]
        return carry

    lax.fori_loop(0, share, one, 0, unroll=min(share, 4))

    for b in range(count):
        both = dot(combine_ref[b], result_ref[b], ((1,), (0,)))
        outs[b][...] = (both[:tokens] + both[tokens:]).astype(jnp.bfloat16)


def expert_blocks(blocks, weights, cap, picks):
    count = len(blocks)
    share, width, rows = weights[0].shape
    experts = WEIGHTS * share
    tokens = (blocks[0].shape[0] - META_ROWS) // (width // LANES) // picks
    shapes = [(tokens, rows)] if count == 1 else [(2, tokens, rows)] + [(tokens, rows)] * (count - 2)
    return pl.pallas_call(
        functools.partial(expert_kernel, count, cap, picks),
        in_specs=[WHOLE] * (count + WEIGHTS),
        out_specs=[WHOLE] * len(shapes),
        out_shape=[jax.ShapeDtypeStruct(shape, jnp.bfloat16) for shape in shapes],
        scratch_shapes=[
            pltpu.VMEM((experts, count * cap, width), jnp.bfloat16),
            pltpu.VMEM((count, 2 * tokens, experts * cap), jnp.bfloat16),
            pltpu.VMEM((count, experts * cap, rows), jnp.bfloat16),
        ],
        compiler_params=pltpu.CompilerParams(vmem_limit_bytes=2 * 3 * experts * cap * width * 2),
        cost_estimate=pl.CostEstimate(
            flops=4 * count * experts * cap * rows * width,
            bytes_accessed=2 * (experts * rows * width + count * tokens * picks * width),
            transcendentals=0,
        ),
        name="experts",
    )(*blocks, *weights)


def place_pieces(sources, pieces, slots_ref):
    n = slots_ref.shape[0]
    here = place_of(lax.axis_index("expert"), n)
    way = 1 - 2 * lax.axis_index("replica")
    for (k, part), piece in zip(sources, pieces):
        slots_ref[at_place((here + way * k + n) % n, n)] = piece[...] if part is None else piece[part]


def collect_kernel(sources, *refs):
    *pieces, slots_ref = refs
    place_pieces(sources, pieces, slots_ref)


def collect(n, sources, pieces):
    return pl.pallas_call(
        functools.partial(collect_kernel, sources),
        in_specs=[WHOLE] * len(pieces),
        out_specs=WHOLE,
        out_shape=jax.ShapeDtypeStruct((n, *pieces[0].shape), jnp.bfloat16),
        compiler_params=pltpu.CompilerParams(vmem_limit_bytes=4 * MIB),
        cost_estimate=pl.CostEstimate(flops=30_000_000_000, bytes_accessed=0, transcendentals=0),
        name="collect",
    )(*pieces)


def join_kernel(sources, held_ref, *refs):
    *pieces, out_ref, slots_ref = refs
    n, _, rows = slots_ref.shape
    slots_ref[...] = held_ref[...]
    place_pieces(sources, pieces, slots_ref)
    for j in range(n):
        out_ref[:, j * rows : (j + 1) * rows] = slots_ref[j]


def join(held, sources, pieces):
    n, tokens, rows = held.shape
    return pl.pallas_call(
        functools.partial(join_kernel, sources),
        in_specs=[WHOLE] * (1 + len(pieces)),
        out_specs=WHOLE,
        out_shape=jax.ShapeDtypeStruct((tokens, n * rows), jnp.bfloat16),
        scratch_shapes=[pltpu.VMEM((n, tokens, rows), jnp.bfloat16)],
        compiler_params=pltpu.CompilerParams(vmem_limit_bytes=4 * MIB),
        name="join",
    )(held, *pieces)


def body(hidden, routes, gates, mantissas, exponents):
    tokens, picks, width = hidden.shape
    n = lax.axis_size("expert")
    owned = mantissas.shape[0]
    experts = 2 * owned
    cap = -(-2 * tokens * picks // experts // 16) * 16
    order = ring_order(n)

    def turn(x, steps, cross=0):
        pairs = [
            (2 * order[i] + core, 2 * order[(i + (1 - 2 * core) * steps) % n] + (core ^ cross))
            for i in range(n)
            for core in range(2)
        ]
        return lax.ppermute(x, ("expert", "replica"), pairs)

    swap = lambda x: lax.ppermute(x, "replica", [(0, 1), (1, 0)])

    exponents = jnp.transpose(exponents, (0, 2, 1))
    hidden2, routes2, gates2 = swap(hidden), swap(routes), swap(gates)
    mine = pack(hidden, routes, gates)
    far = n // 2
    first, second = [mine], [pack(hidden2, routes2, gates2)]
    half = owned // 2
    theirs, exponents2, exponents, *_ = after((mantissas, exponents, exponents, mine, hidden2, routes2, gates2))
    theirs, exponents2 = swap(theirs), swap(exponents2)
    own1 = decode(mantissas, exponents, 0, half, 48 * MIB)
    own2 = decode(mantissas, exponents, half, owned - half, 48 * MIB)
    homes = []

    for k in range(1, far):
        first.append(turn(first[k - 1], 1))
        second.append(turn(second[k - 1], 1))
        if k == 1:
            first[1], own1, own2 = after((first[1], own1, own2))
            theirs, exponents2, _ = after((theirs, exponents2, first[1]))
            other1 = decode(theirs, exponents2, 0, half, 24 * MIB)
            other2 = decode(theirs, exponents2, half, owned - half, 24 * MIB)
            weights = [own1, own2, other1, other2]
            second[1], other1, other2 = after((second[1], other1, other2))
        else:
            blocks = [first[k - 1], second[k - 1]] + [mine] * (k == 2)
            pair, *own = expert_blocks(blocks, weights, cap, picks)
            first[k], weights[0], _ = after((first[k], weights[0], pair))
            homes.append(pair)
            if own:
                (local,) = own
    last = turn(first[-1], 1)
    (pair,) = expert_blocks([first[-1], second[-1]], weights, cap, picks)
    homes = after((*homes, pair))
    homes = [turn(home, -k) for k, home in enumerate(homes, 1)]
    weights[0] = after((weights[0], pair))[0]
    (out,) = expert_blocks([last], weights, cap, picks)
    gone = turn(out, far)
    homes = after((out, *homes))[1:]
    steps = range(1, far)
    held = collect(n, [(far, None), (0, None)] + [(k, 0) for k in steps], [gone, local, *homes])
    return join(held, [(-k, 1) for k in steps], [swap(home) for home in homes])


def solution(mesh):
    return jax.shard_map(
        body,
        mesh=mesh,
        in_specs=(
            P(("groups", "expert", "replica"), None, None),
            P(("groups", "expert", "replica"), None),
            P(("groups", "expert", "replica"), None),
            P("replica", "expert", None),
            P("replica", "expert", None),
        ),
        out_specs=P(("groups", "expert", "replica"), None),
        check_vma=False,
    )
```
